32 devices in a mesh: bin: 16 (over z, x, core), diag: 2 (over y).
Axes of the slice: x: 2, y: 2, z: 4, core: 2. Of those that a mesh axis runs over, the one named last changes fastest.
Arguments:
- embeddings: bfloat16 [256, 6144], P('diag', 'bin'), may hold values from -6 to 6
- projection: bfloat16 [256, 64], P('diag'), may hold values from -0.375 to 0.375
- dist_bias: float32 [32, 256], replicated, may hold values from -3 to 3
- conv_weight: bfloat16 [2, 9, 32, 32], replicated, may hold values from -0.375 to 0.375
- head_weight: float32 [32], replicated, may hold values from -1 to 1
- dilations: int32 [2], replicated, may hold values from 1 to 4, as said below
- band_limit: int32 [6144], P('bin'), may hold values from 64 to 256
- cotangent: float32 [256, 6144], P('diag', 'bin'), may hold values from -6 to 6
Outputs:
- predicted: float32 [256, 6144], P('diag', 'bin')
- grad_embed: float32 [256, 6144], P('diag', 'bin')
- grad_proj: float32 [256, 64], P('diag')
- grad_conv: float32 [2, 9, 32, 32], replicated
The draws below stay inside these ranges and needn't reach their ends.
Inputs may be any that keep to these rules, and one draw needn't show every extreme that they name: `dilations`: one of the 2 layers has dilation exactly 4.
All inputs are finite; a program needn't handle non-finite values.
Results may differ from the reference program's by a relative error of at most 0.0059.
Values may be sent and summed in bfloat16 or wider, within the bound.
A program may use at most 256 MiB of HBM per device.

```python
import math
import jax
import jax.numpy as jnp
from jax import lax

BIN_DEV = 384
DIAGS = 256
CHAN = 32
EMBED = 256
MAXDIL = 4
LAYERS = 2
BINS = 6144
N_BIN = 16


def draw_dilations(key, part):
    key = jax.random.fold_in(key, 11)
    first_key, second_key = jax.random.split(key)
    position = jax.random.randint(first_key, (), 0, 2)
    others = jax.random.randint(second_key, (2,), 1, MAXDIL + 1)
    return jnp.where(jnp.arange(2) == position, MAXDIL, others).astype(jnp.int32)


def plant(array, stream_key, low, high):
    dims = array.shape
    spot = [jax.random.randint(jax.random.fold_in(stream_key, axis), (), 0, dims[axis]) for axis in range(len(dims))]
    array = array.at[tuple(spot)].set(low)
    longest = dims.index(max(dims))
    spot[longest] = (spot[longest] + 1) % dims[longest]
    return array.at[tuple(spot)].set(high)


def block_scale(stream_key, extent, cuts, smallest, high):
    level, own = 1.0, jax.random.fold_in(stream_key, 6)
    for axis_at, blocks in cuts:
        draws = jnp.exp(jax.random.uniform(jax.random.fold_in(own, axis_at), (blocks,), jnp.float32, smallest / len(cuts), high / len(cuts)))
        level = level * jnp.repeat(draws, extent[axis_at] // blocks).reshape([-1 if axis == axis_at else 1 for axis in range(len(extent))])
    return level


def centred(rng, shape, spread, most, shards=(), kind=jnp.bfloat16):
    drawn = spread * jax.random.normal(rng, shape, jnp.float32)
    if shards:
        drawn = drawn * block_scale(rng, shape, shards, -0.22, 0.18)
    return jnp.clip(drawn, -most, most).astype(kind)


def setup_inputs(seed: int = 0) -> dict:
    seeds = jax.random.split(jax.random.key(seed), 9)
    return {
        "embeddings": centred(seeds[0], (EMBED, BINS), 1.0, 6.0, ((0, 2), (1, 16))),
        "projection": centred(seeds[1], (EMBED, 2 * CHAN), EMBED ** -0.5, 0.375, ((0, 2),)),
        "dist_bias": centred(seeds[2], (CHAN, DIAGS), 0.5, 3.0, (), jnp.float32),
        "conv_weight": centred(seeds[3], (LAYERS, 9, CHAN, CHAN), (9 * CHAN) ** -0.5, 0.375),
        "head_weight": centred(seeds[4], (CHAN,), CHAN ** -0.5, 1.0, (), jnp.float32),
        "dilations": draw_dilations(jax.random.fold_in(seeds[8], 71), 0),
        "band_limit": plant(jax.random.randint(seeds[6], (BINS,), DIAGS // 4, DIAGS + 1), jax.random.fold_in(seeds[6], 1), DIAGS // 4, DIAGS).astype(jnp.int32),
        "cotangent": centred(seeds[7], (DIAGS, BINS), 1.0, 6.0, ((0, 2), (1, 16)), jnp.float32),
    }


HIGHEST = lax.Precision.HIGHEST

def skew_read(window, diag_count, row_count):
    channels = window.shape[0]
    span_len = row_count + diag_count - 1
    tiled_rows = jnp.broadcast_to(window[:, None, :], (channels, diag_count, span_len)).reshape(channels, diag_count * span_len)
    tiled_rows = jnp.pad(tiled_rows, ((0, 0), (0, diag_count)))
    return tiled_rows.reshape(channels, diag_count, span_len + 1)[:, :, :row_count]

def skew_write(values):
    channels, diag_count, row_count = values.shape
    span_len = row_count + diag_count - 1
    padded = jnp.pad(values, ((0, 0), (0, 0), (0, span_len + 1 - row_count)))
    flat_view = padded.reshape(channels, diag_count * (span_len + 1))[:, :diag_count * span_len]
    return lax.optimization_barrier(jnp.sum(flat_view.reshape(channels, diag_count, span_len), axis=1))

def tap_slice(padded, diag_start, row_start, diag_count, row_count):
    return lax.dynamic_slice(padded, (jnp.int32(0), diag_start.astype(jnp.int32), row_start.astype(jnp.int32)), (padded.shape[0], diag_count, row_count))

def conv_forward(padded, weight, dilation, diag_count, row_count, margin):
    summed = jnp.zeros((weight.shape[1], diag_count, row_count), jnp.float32)
    for kernel_tap in range(9):
        along_bin = kernel_tap // 3 - 1
        along_diag = kernel_tap % 3 - 1
        sliced = tap_slice(padded, margin + along_diag * dilation, margin + along_bin * dilation, diag_count, row_count)
        summed = summed + jnp.einsum('oc,cdi->odi', weight[kernel_tap].astype(jnp.float32), sliced.astype(jnp.float32), precision=HIGHEST)
    return summed

def conv_transpose(padded, weight, dilation, diag_count, row_count, margin):
    summed = jnp.zeros((weight.shape[2], diag_count, row_count), jnp.float32)
    for kernel_tap in range(9):
        along_bin = kernel_tap // 3 - 1
        along_diag = kernel_tap % 3 - 1
        sliced = tap_slice(padded, margin - along_diag * dilation, margin - along_bin * dilation, diag_count, row_count)
        summed = summed + jnp.einsum('oc,odi->cdi', weight[kernel_tap].astype(jnp.float32), sliced.astype(jnp.float32), precision=HIGHEST)
    return summed

def weight_grad(grad_values, padded, dilation, diag_count, row_count, margin):
    results = []
    for kernel_tap in range(9):
        along_bin = kernel_tap // 3 - 1
        along_diag = kernel_tap % 3 - 1
        sliced = tap_slice(padded, margin + along_diag * dilation, margin + along_bin * dilation, diag_count, row_count)
        results.append(jnp.einsum('odi,cdi->oc', grad_values.astype(jnp.float32), sliced.astype(jnp.float32), precision=HIGHEST))
    return jnp.stack(results)

def reference(embeddings, projection, dist_bias, conv_weight, head_weight, dilations, band_limit, cotangent):
    margin = MAXDIL
    inner = 4 * margin
    region = BIN_DEV + 8 * margin
    projected = jnp.einsum('ek,eb->kb', projection.astype(jnp.float32), embeddings.astype(jnp.float32), precision=HIGHEST)
    left_padded = jnp.pad(projected[:CHAN], ((0, 0), (inner, inner)))
    right_padded = jnp.pad(projected[CHAN:], ((0, 0), (inner, DIAGS + inner)))
    limit_padded = jnp.pad(band_limit, (inner, inner))
    cot_padded = jnp.pad(cotangent, ((0, 0), (inner, inner)))
    bias_cols = dist_bias.astype(jnp.float32)[:, :, None]
    head_vector = head_weight.astype(jnp.float32)
    diag_ids = jnp.arange(DIAGS, dtype=jnp.int32)[:, None]
    anchor = jnp.int32(0)
    dilation_one = dilations[0]
    dilation_two = dilations[1]
    weight_one = conv_weight[0]
    weight_two = conv_weight[1]

    def widened(values):
        return jnp.pad(values, ((0, 0), (margin, margin), (margin, margin)))

    def block(carried, block_index):
        wgrad_sum, grad_right = carried
        first_row = (block_index * BIN_DEV).astype(jnp.int32)
        row_ids = first_row - inner + jnp.arange(region, dtype=jnp.int32)[None, :]
        left_rows = lax.dynamic_slice(left_padded, (anchor, first_row), (CHAN, region))
        right_rows = lax.dynamic_slice(right_padded, (anchor, first_row), (CHAN, region + DIAGS - 1))
        limit_rows = lax.dynamic_slice(limit_padded, (first_row,), (region,))
        cot_rows = lax.dynamic_slice(cot_padded, (anchor, first_row), (DIAGS, region))
        inside = (row_ids >= 0) & (row_ids < BINS) & (row_ids + diag_ids < BINS)
        inside_mask = inside.astype(jnp.float32)
        counted_mask = (inside & (diag_ids < limit_rows[None, :])).astype(jnp.float32)
        tanh_zero = jnp.tanh(left_rows[:, None, :] + skew_read(right_rows, DIAGS, region) + bias_cols)
        pair_zero = (inside_mask * tanh_zero).astype(jnp.bfloat16)
        padded_zero = widened(pair_zero)
        act_one = conv_forward(padded_zero, weight_one, dilation_one, DIAGS, region, margin)
        tanh_one = jnp.tanh(act_one)
        pair_one = (inside_mask * (pair_zero.astype(jnp.float32) + tanh_one)).astype(jnp.bfloat16)
        padded_one = widened(pair_one)
        tanh_two = jnp.tanh(conv_forward(padded_one, weight_two, dilation_two, DIAGS, region, margin))
        predicted = counted_mask * jnp.einsum('c,cdi->di', head_vector, tanh_two, precision=HIGHEST)
        grad_two = ((cot_rows * counted_mask)[None, :, :] * head_vector[:, None, None] * (1.0 - tanh_two * tanh_two)).astype(jnp.bfloat16)
        wgrad_two = weight_grad(grad_two[:, :, inner:inner + BIN_DEV], padded_one[:, :, inner:inner + BIN_DEV + 2 * margin], dilation_two, DIAGS, BIN_DEV, margin)
        back_one = conv_transpose(widened(grad_two), weight_two, dilation_two, DIAGS, region, margin)
        grad_one = (back_one * inside_mask * (1.0 - tanh_one * tanh_one)).astype(jnp.bfloat16)
        wgrad_one = weight_grad(grad_one[:, :, inner:inner + BIN_DEV], padded_zero[:, :, inner:inner + BIN_DEV + 2 * margin], dilation_one, DIAGS, BIN_DEV, margin)
        back_zero = inside_mask * back_one + conv_transpose(widened(grad_one), weight_one, dilation_one, DIAGS, region, margin)
        grad_pre = (back_zero * inside_mask * (1.0 - tanh_zero * tanh_zero))[:, :, inner:inner + BIN_DEV]
        grad_left = lax.optimization_barrier(jnp.sum(grad_pre, axis=1))
        spilled = skew_write(grad_pre)
        current = lax.dynamic_slice(grad_right, (anchor, first_row), (CHAN, BIN_DEV + DIAGS - 1))
        grad_right = lax.dynamic_update_slice(grad_right, current + spilled, (anchor, first_row))
        wgrad_sum = wgrad_sum + jnp.stack([wgrad_one, wgrad_two])
        return ((wgrad_sum, grad_right), (predicted[:, inner:inner + BIN_DEV], grad_left))
    start_carry = (jnp.zeros((LAYERS, 9, CHAN, CHAN), jnp.float32), jnp.zeros((CHAN, BINS + DIAGS), jnp.float32))
    (wgrad_sum, grad_right), (pred_blocks, left_blocks) = lax.scan(block, start_carry, jnp.arange(N_BIN, dtype=jnp.int32))
    predicted = jnp.transpose(pred_blocks, (1, 0, 2)).reshape(DIAGS, BINS)
    grad_left = jnp.transpose(left_blocks, (1, 0, 2)).reshape(CHAN, BINS)
    grad_both = jnp.concatenate([grad_left, grad_right[:, :BINS]], axis=0)
    scaling = 1.0 / math.sqrt(BINS * DIAGS)
    grad_embed = jnp.einsum('ek,kb->eb', projection.astype(jnp.float32), grad_both, precision=HIGHEST)
    grad_proj = scaling * jnp.einsum('eb,kb->ek', embeddings.astype(jnp.float32), grad_both, precision=HIGHEST)
    grad_conv = scaling * wgrad_sum
    return (predicted, grad_embed, grad_proj, grad_conv)
```

```python
import functools
import math

import jax
import jax.numpy as jnp
from jax import lax
from jax.experimental import pallas as pl
from jax.experimental.pallas import tpu as pltpu
from jax.sharding import PartitionSpec as P

MAXDIL = 4
HALO = 4 * MAXDIL
PACK = 8


HIGHEST = lax.Precision.HIGHEST


def cut(rows, most):
    return max(n for n in range(1, most + 1) if rows % n == 0)


def kernel(
    plan, info, left, right, bias, mats, expand, head, cots, pred, grad_left, grad_right, wgrad,
    x0, h0, s0, x1, h1, s1, g2, hg2, b1, wacc,
):
    sub, groups, total, n1, n2, n3, n4 = plan
    lanes = 256
    first = info[2]
    dil_one, dil_two = info[0], info[1]
    g_ids = lax.broadcasted_iota(jnp.int32, (groups, lanes), 0)
    diag_ids = g_ids * PACK + lax.shift_right_logical(
        lax.broadcasted_iota(jnp.int32, (groups, lanes), 1), 5
    )

    def inside_rows(start, count):
        rows = first + start + lax.broadcasted_iota(jnp.int32, (count, 1, 1), 0)
        bound = jnp.where(rows >= 0, total - rows, 0)
        return (diag_ids[None] < bound).reshape(count * groups, lanes)

    def store(x_ref, h_ref, start, count, value):
        value = value.astype(jnp.bfloat16).astype(jnp.float32)
        x_ref[pl.ds(start, count)] = value.astype(jnp.bfloat16).reshape(count, groups, lanes)
        size = count * groups
        g_row = lax.broadcasted_iota(jnp.int32, (count, groups, 128), 1).reshape(size, 128)
        below = jnp.where(g_row == 0, 0.0, pltpu.roll(value[:, 128:], 1, 0))
        above = jnp.where(g_row == groups - 1, 0.0, pltpu.roll(value[:, :128], size - 1, 0))
        h_ref[pl.ds(start, count), :, :128] = below.astype(jnp.bfloat16).reshape(
            count, groups, 128
        )
        h_ref[pl.ds(start, count), :, 128:] = above.astype(jnp.bfloat16).reshape(
            count, groups, 128
        )

    def taps(x_ref, h_ref, start, count, step):
        pieces = []
        for along in (-1, 0, 1):
            at = start + along * step
            pieces.append(x_ref[pl.ds(at, count)].reshape(count * groups, lanes))
            pieces.append(h_ref[pl.ds(at, count)].reshape(count * groups, lanes))
        return jnp.concatenate(pieces, axis=1)

    def conv(x_ref, h_ref, mat, start, count, step):
        return jnp.dot(
            taps(x_ref, h_ref, start, count, step),
            mats[mat],
            preferred_element_type=jnp.float32,
        )

    n0 = 4

    @pl.loop(0, (sub + 2 * HALO) // n0)
    def _(block):
        start = block * n0
        rows = []
        for u in range(n0):
            at = start + u
            halves = []
            for half in range(2):
                partner = right[half, pl.ds(at, groups, stride=PACK), :]
                halves.append(partner + left[half, pl.ds(at, 1), :])
            rows.append(jnp.concatenate(halves, axis=1) + bias[...])
        t = jnp.tanh(jnp.concatenate(rows, axis=0))
        keep = inside_rows(start, n0)
        s0[pl.ds(start, n0)] = (
            jnp.where(keep, 1.0 - t * t, 0.0).astype(jnp.bfloat16).reshape(n0, groups, lanes)
        )
        store(x0, h0, start, n0, jnp.where(keep, t, 0.0))

    @pl.loop(0, (sub + 6 * MAXDIL) // n1)
    def _(block):
        start = MAXDIL + block * n1
        t = jnp.tanh(conv(x0, h0, 0, start, n1, dil_one))
        keep = inside_rows(start, n1)
        s1[pl.ds(start, n1)] = (
            jnp.where(keep, 1.0 - t * t, 0.0).astype(jnp.bfloat16).reshape(n1, groups, lanes)
        )
        before = x0[pl.ds(start, n1)].reshape(n1 * groups, lanes).astype(jnp.float32)
        store(x1, h1, start, n1, jnp.where(keep, before + t, 0.0))

    @pl.loop(0, (sub + 4 * MAXDIL) // n2)
    def _(block):
        start = 2 * MAXDIL + block * n2
        t = jnp.tanh(conv(x1, h1, 1, start, n2, dil_two))
        scored = lax.dot_general(
            head[...], t.astype(jnp.bfloat16), (((1,), (1,)), ((), ())),
            preferred_element_type=jnp.float32,
        )
        pred[block] = scored[:PACK] + scored[PACK:]
        factor = lax.dot_general(
            cots[block], expand[...], (((0,), (0,)), ((), ())),
            preferred_element_type=jnp.float32,
        )
        store(g2, hg2, start, n2, factor * (1.0 - t * t))

    def weight_grad(layer, g_ref, x_ref, h_ref, step):
        wacc[...] = jnp.zeros_like(wacc)

        @pl.loop(0, sub // n4)
        def _(block):
            start = HALO + block * n4
            wacc[...] += lax.dot_general(
                g_ref[pl.ds(start, n4)].reshape(n4 * groups, lanes),
                taps(x_ref, h_ref, start, n4, step),
                (((0,), (0,)), ((), ())),
                preferred_element_type=jnp.float32,
            )

        width = 2 * lanes
        out_diag = lax.shift_right_logical(
            lax.broadcasted_iota(jnp.int32, (lanes, width), 0), 5
        )
        slot = lax.shift_right_logical(lax.broadcasted_iota(jnp.int32, (lanes, width), 1), 5)
        in_diag = jnp.where(slot < 8, slot, jnp.where(slot < 12, slot - 12, slot - 4))
        fold = (
            lax.broadcasted_iota(jnp.int32, (width, 32), 0) & 31
            == lax.broadcasted_iota(jnp.int32, (width, 32), 1)
        ).astype(jnp.float32)
        for a in range(3):
            product = wacc[:, a * width : (a + 1) * width]
            for b in range(3):
                picked = jnp.where(in_diag == out_diag + (b - 1) * step, product, 0.0)
                total_rows = picked[:32]
                for d in range(1, PACK):
                    total_rows = total_rows + picked[32 * d : 32 * (d + 1)]
                wgrad[layer, 3 * a + b] = jnp.dot(
                    total_rows, fold, precision=HIGHEST, preferred_element_type=jnp.float32
                )

    weight_grad(1, g2, x1, h1, dil_two)

    @pl.loop(0, (sub + 2 * MAXDIL) // n3)
    def _(block):
        start = 3 * MAXDIL + block * n3
        back = conv(g2, hg2, 2, start, n3, dil_two)
        b1[pl.ds(start, n3)] = back.reshape(n3, groups, lanes)
        scale = s1[pl.ds(start, n3)].reshape(n3 * groups, lanes).astype(jnp.float32)
        store(x1, h1, start, n3, back * scale)

    weight_grad(0, x1, x0, h0, dil_one)
    grad_right[...] = jnp.zeros_like(grad_right)

    @pl.loop(0, sub // n4)
    def _(block):
        start = HALO + block * n4
        back = conv(x1, h1, 3, start, n4, dil_one)
        scale = s0[pl.ds(start, n4)].reshape(n4 * groups, lanes).astype(jnp.float32)
        grad = (back + b1[pl.ds(start, n4)].reshape(n4 * groups, lanes)) * scale
        grad_left[block] = jnp.sum(grad.reshape(n4, groups, lanes), axis=1)
        for u in range(n4):
            at = pl.ds(block * n4 + u, groups, stride=PACK)
            for half in range(2):
                piece = grad[u * groups : (u + 1) * groups, 128 * half : 128 * (half + 1)]
                grad_right[half, at, :] = grad_right[half, at, :] + piece


def tap_matrix(weight, dilation, sign):
    diags = jnp.array([0, 1, 2, 3, 4, 5, 6, 7, -4, -3, -2, -1, 8, 9, 10, 11], jnp.int32)
    outs, ins = weight.shape[1], weight.shape[2]
    weight = weight.reshape(3, 3, outs, ins)
    if sign < 0:
        weight = weight[::-1]
    total = jnp.zeros((3, 16, ins, PACK, outs), weight.dtype)
    for b in range(3):
        hit = diags[:, None] == jnp.arange(PACK)[None, :] + sign * (b - 1) * dilation
        spread = jnp.transpose(weight[:, b], (0, 2, 1))[:, None, :, None, :]
        total = jnp.where(hit[None, :, None, :, None], spread, total)
    return total.reshape(3 * 16 * ins, PACK * outs)


def split_two(x):
    high = x.astype(jnp.bfloat16)
    return high, (x - high.astype(jnp.float32)).astype(jnp.bfloat16)


def shifted(axis, size, by):
    return [(i, i + by) for i in range(size) if 0 <= i + by < size]


def on_device(
    embeddings, projection, dist_bias, conv_weight, head_weight, dilations, band_limit, cotangent
):
    channels = conv_weight.shape[2]
    diag_dev, rows_dev = cotangent.shape
    n_bin, n_diag = lax.axis_size("bin"), lax.axis_size("diag")
    total_bins, diags = rows_dev * n_bin, diag_dev * n_diag
    me = lax.axis_index("diag")
    first_row = lax.axis_index("bin") * rows_dev
    sub = rows_dev // n_diag
    groups = diags // PACK
    lanes = PACK * channels
    reach = HALO + diags

    def around(block, before, after):
        low = lax.ppermute(block[:, rows_dev - before :], "bin", shifted("bin", n_bin, 1))
        high = lax.ppermute(block[:, :after], "bin", shifted("bin", n_bin, -1))
        return jnp.concatenate([low, block, high], axis=1)

    def pairs(k):
        return [(i, (i + k) % n_diag) for i in range(n_diag)]

    wide = around(embeddings, HALO, reach)
    part = jnp.einsum("eb,ek->bk", wide, projection, preferred_element_type=jnp.float32)
    span = sub + HALO + reach
    projected = lax.dynamic_slice_in_dim(part, me * sub, span, 0)
    for k in range(1, n_diag):
        other = lax.rem(me + k, n_diag)
        projected = projected + lax.ppermute(
            lax.dynamic_slice_in_dim(part, other * sub, span, 0), "diag", pairs(k)
        )
    region = sub + 2 * HALO
    reads = region + PACK * (groups - 1)
    left = jnp.tile(projected[:region, :channels], (1, PACK))
    right = jnp.concatenate(
        [projected[d : d + reads, channels:] for d in range(PACK)], axis=1
    )
    halves = lambda x: jnp.stack([x[:, : lanes // 2], x[:, lanes // 2 :]])
    bias = jnp.transpose(dist_bias.reshape(channels, groups, PACK), (1, 2, 0)).reshape(
        groups, lanes
    )

    row_ids = first_row + jnp.arange(rows_dev, dtype=jnp.int32)[None, :]
    diag_ids = me * diag_dev + jnp.arange(diag_dev, dtype=jnp.int32)[:, None]
    counted = (row_ids + diag_ids < total_bins) & (diag_ids < band_limit[None, :])
    margin = 2 * MAXDIL
    cot_wide = around(jnp.where(counted, cotangent, 0.0), margin, margin)
    cot_span = sub + 2 * margin
    cot = jnp.zeros((n_diag, diag_dev, cot_span), jnp.float32)
    for k in range(n_diag):
        other = lax.rem(me + k, n_diag)
        piece = lax.dynamic_slice_in_dim(cot_wide, other * sub, cot_span, 1)
        if k:
            piece = lax.ppermute(piece, "diag", pairs(k))
        cot = lax.dynamic_update_index_in_dim(cot, piece, lax.rem(me - k + n_diag, n_diag), 0)
    n1 = cut(sub + 6 * MAXDIL, 24)
    n2 = cut(cot_span, 16)
    n3 = cut(sub + 2 * MAXDIL, 25)
    n4 = cut(sub, 24)
    blocks = cot_span // n2
    cot = jnp.transpose(cot.reshape(groups, PACK, blocks, n2), (2, 1, 3, 0)).reshape(
        blocks, PACK, n2 * groups
    )
    cot_high, cot_low = split_two(cot)
    head_high, head_low = split_two(head_weight)
    eye = jnp.eye(PACK, dtype=jnp.bfloat16)
    spread = lambda h: (eye[:, :, None] * h[None, None, :]).reshape(PACK, lanes)
    pad = jnp.zeros((PACK, lanes), jnp.bfloat16)
    cots = jnp.concatenate([cot_high, cot_low, cot_high, jnp.zeros_like(cot_high)], axis=1)
    expand = jnp.concatenate([spread(head_high), spread(head_high), spread(head_low), pad])
    head = jnp.concatenate([spread(head_high), spread(head_low)])
    mats = jnp.stack(
        [
            tap_matrix(conv_weight[0], dilations[0], 1),
            tap_matrix(conv_weight[1], dilations[1], 1),
            tap_matrix(jnp.transpose(conv_weight[1], (0, 2, 1)), dilations[1], -1),
            tap_matrix(jnp.transpose(conv_weight[0], (0, 2, 1)), dilations[0], -1),
        ]
    )
    info = jnp.concatenate([dilations, (first_row + me * sub - HALO)[None].astype(jnp.int32)])

    writes = sub + PACK * (groups - 1)
    vmem = pl.BlockSpec(memory_space=pltpu.VMEM)
    half_map = pltpu.VMEM((region, groups, lanes), jnp.bfloat16)
    pred, grad_left, grad_right, conv_part = pl.pallas_call(
        functools.partial(kernel, (sub, groups, total_bins, n1, n2, n3, n4)),
        out_shape=[
            jax.ShapeDtypeStruct((blocks, PACK, n2 * groups), jnp.float32),
            jax.ShapeDtypeStruct((sub // n4, n4, lanes), jnp.float32),
            jax.ShapeDtypeStruct((2, writes, lanes // 2), jnp.float32),
            jax.ShapeDtypeStruct(conv_weight.shape, jnp.float32),
        ],
        in_specs=[pl.BlockSpec(memory_space=pltpu.SMEM)] + [vmem] * 7,
        out_specs=[vmem] * 4,
        scratch_shapes=[half_map] * 8
        + [
            pltpu.VMEM((region, groups, lanes), jnp.float32),
            pltpu.VMEM((lanes, 6 * lanes), jnp.float32),
        ],
        compiler_params=pltpu.CompilerParams(vmem_limit_bytes=60 * 1024 * 1024),
        name="band",
    )(info, halves(left), halves(right), bias, mats, expand, head, cots)

    conv_sum = lax.psum(conv_part, ("bin", "diag"))

    grad_right = jnp.concatenate([grad_right[0], grad_right[1]], axis=1)
    spilled = jnp.zeros((sub + diags, channels), jnp.float32)
    for d in range(PACK):
        spilled = spilled + jnp.pad(
            grad_right[:, d * channels : (d + 1) * channels],
            ((d, sub + diags - writes - d), (0, 0)),
        )
    lefts = jnp.sum(grad_left.reshape(sub, PACK, channels), axis=1)
    own = jnp.concatenate([jnp.pad(lefts, ((0, diags), (0, 0))), spilled], axis=1)
    buffer = lax.dynamic_update_slice_in_dim(
        jnp.zeros((rows_dev + diags, 2 * channels), jnp.float32), own, me * sub, 0
    )
    both = buffer
    for k in range(1, n_diag):
        both = both + lax.ppermute(buffer, "diag", pairs(k))
    incoming = lax.ppermute(both[rows_dev:, channels:], "bin", shifted("bin", n_bin, 1))
    both = both[:rows_dev] + jnp.pad(incoming, ((0, rows_dev - diags), (channels, 0)))
    grad_embed = jnp.einsum(
        "ek,bk->eb", projection.astype(jnp.float32), both, precision=HIGHEST
    )
    proj_part = jnp.einsum(
        "eb,bk->ek", embeddings.astype(jnp.float32), both, precision=HIGHEST
    )
    proj_sum = lax.psum(proj_part, "bin")

    pred = jnp.transpose(pred.reshape(blocks, PACK, n2, groups), (3, 1, 0, 2)).reshape(
        diags, cot_span
    )[:, margin : margin + sub]
    pred_local = jnp.zeros((diag_dev, rows_dev), jnp.float32)
    for k in range(n_diag):
        other = lax.rem(me + k, n_diag)
        piece = lax.dynamic_slice_in_dim(pred, other * diag_dev, diag_dev, 0)
        if k:
            piece = lax.ppermute(piece, "diag", pairs(k))
        pred_local = lax.dynamic_update_slice_in_dim(
            pred_local, piece, lax.rem(me - k + n_diag, n_diag) * sub, 1
        )
    pred_local = jnp.where(counted, pred_local, 0.0)
    scaling = 1.0 / math.sqrt(total_bins * diags)
    return (pred_local, grad_embed, scaling * proj_sum, scaling * conv_sum)


def solution(mesh):
    return jax.shard_map(
        on_device,
        mesh=mesh,
        in_specs=(
            P("diag", "bin"),
            P("diag", None),
            P(),
            P(),
            P(),
            P(),
            P("bin"),
            P("diag", "bin"),
        ),
        out_specs=(P("diag", "bin"), P("diag", "bin"), P("diag", None), P()),
        check_vma=False,
    )
```

```python
import functools
import math

import jax
import jax.numpy as jnp
from jax import lax
from jax.experimental import pallas as pl
from jax.experimental.pallas import tpu as pltpu
from jax.sharding import PartitionSpec as P

MAXDIL = 4
HALO = 4 * MAXDIL
PACK = 8


HIGHEST = lax.Precision.HIGHEST


def cut(rows, most):
    return max(n for n in range(1, most + 1) if rows % n == 0)


def kernel(
    plan, info, left, right, bias, weights, expand, head, cots, pred, grad_left, grad_right,
    wgrad, x0, h0, s0, x1, h1, s1, g2, hg2, b1, wacc, mats,
):
    sub, groups, total, n1, n2, n3, n4 = plan
    lanes = 256
    first = info[2]
    dil_one, dil_two = info[0], info[1]
    g_ids = lax.broadcasted_iota(jnp.int32, (groups, lanes), 0)
    diag_ids = g_ids * PACK + lax.shift_right_logical(
        lax.broadcasted_iota(jnp.int32, (groups, lanes), 1), 5
    )

    def inside_rows(start, count):
        rows = first + start + lax.broadcasted_iota(jnp.int32, (count, 1, 1), 0)
        bound = jnp.where(rows >= 0, total - rows, 0)
        return (diag_ids[None] < bound).reshape(count * groups, lanes)

    def store(x_ref, h_ref, start, count, value):
        value = value.astype(jnp.bfloat16).astype(jnp.float32)
        x_ref[pl.ds(start, count)] = value.astype(jnp.bfloat16).reshape(count, groups, lanes)
        size = count * groups
        g_row = lax.broadcasted_iota(jnp.int32, (count, groups, 128), 1).reshape(size, 128)
        below = jnp.where(g_row == 0, 0.0, pltpu.roll(value[:, 128:], 1, 0))
        above = jnp.where(g_row == groups - 1, 0.0, pltpu.roll(value[:, :128], size - 1, 0))
        h_ref[pl.ds(start, count), :, :128] = below.astype(jnp.bfloat16).reshape(
            count, groups, 128
        )
        h_ref[pl.ds(start, count), :, 128:] = above.astype(jnp.bfloat16).reshape(
            count, groups, 128
        )

    def taps(x_ref, h_ref, start, count, step):
        pieces = []
        for along in (-1, 0, 1):
            at = start + along * step
            pieces.append(x_ref[pl.ds(at, count)].reshape(count * groups, lanes))
            pieces.append(h_ref[pl.ds(at, count)].reshape(count * groups, lanes))
        return jnp.concatenate(pieces, axis=1)

    def conv(x_ref, h_ref, mat, start, count, step):
        return jnp.dot(
            taps(x_ref, h_ref, start, count, step),
            mats[mat],
            preferred_element_type=jnp.float32,
        )

    width = 2 * lanes

    def diag_of(slot):
        return jnp.where(slot < 8, slot, jnp.where(slot < 12, slot - 12, slot - 4))

    delta = diag_of(
        lax.shift_right_logical(lax.broadcasted_iota(jnp.int32, (width, lanes), 0), 5)
    ) - lax.shift_right_logical(lax.broadcasted_iota(jnp.int32, (width, lanes), 1), 5)
    repeat = (
        lax.broadcasted_iota(jnp.int32, (32, lanes), 0)
        == lax.broadcasted_iota(jnp.int32, (32, lanes), 1) & 31
    ).astype(jnp.bfloat16)
    for mat, layer, sign, step in (
        (0, 0, 1, dil_one), (1, 1, 1, dil_two), (2, 1, -1, dil_two), (3, 0, -1, dil_one)
    ):
        for along in range(3):
            taken = along if sign > 0 else 2 - along
            total_mat = jnp.zeros((width, lanes), jnp.float32)
            for b in range(3):
                spread = lax.dot_general(
                    weights[layer, 3 * taken + b], repeat,
                    (((0 if sign > 0 else 1,), (0,)), ((), ())),
                    preferred_element_type=jnp.float32,
                )
                total_mat = jnp.where(
                    delta == sign * (b - 1) * step,
                    jnp.concatenate([spread] * 16, axis=0),
                    total_mat,
                )
            mats[mat, along * width : (along + 1) * width] = total_mat.astype(jnp.bfloat16)

    n0 = 4

    @pl.loop(0, (sub + 2 * HALO) // n0)
    def _(block):
        start = block * n0
        rows = []
        for u in range(n0):
            at = start + u
            halves = []
            for half in range(2):
                partner = right[half, pl.ds(at, groups, stride=PACK), :]
                halves.append(partner + left[half, pl.ds(at, 1), :])
            rows.append(jnp.concatenate(halves, axis=1) + bias[...])
        t = jnp.tanh(jnp.concatenate(rows, axis=0))
        keep = inside_rows(start, n0)
        s0[pl.ds(start, n0)] = (
            jnp.where(keep, 1.0 - t * t, 0.0).astype(jnp.bfloat16).reshape(n0, groups, lanes)
        )
        store(x0, h0, start, n0, jnp.where(keep, t, 0.0))

    @pl.loop(0, (sub + 6 * MAXDIL) // n1)
    def _(block):
        start = MAXDIL + block * n1
        t = jnp.tanh(conv(x0, h0, 0, start, n1, dil_one))
        keep = inside_rows(start, n1)
        s1[pl.ds(start, n1)] = (
            jnp.where(keep, 1.0 - t * t, 0.0).astype(jnp.bfloat16).reshape(n1, groups, lanes)
        )
        before = x0[pl.ds(start, n1)].reshape(n1 * groups, lanes).astype(jnp.float32)
        store(x1, h1, start, n1, jnp.where(keep, before + t, 0.0))

    @pl.loop(0, (sub + 4 * MAXDIL) // n2)
    def _(block):
        start = 2 * MAXDIL + block * n2
        t = jnp.tanh(conv(x1, h1, 1, start, n2, dil_two))
        t_high = t.astype(jnp.bfloat16)
        t_low = (t - t_high.astype(jnp.float32)).astype(jnp.bfloat16)
        scored = lax.dot_general(
            head[...], t_high, (((1,), (1,)), ((), ())), preferred_element_type=jnp.float32
        ) + lax.dot_general(
            head[...], t_low, (((1,), (1,)), ((), ())), preferred_element_type=jnp.float32
        )
        pred[block] = scored[:PACK] + scored[PACK:]
        factor = lax.dot_general(
            cots[block], expand[...], (((0,), (0,)), ((), ())),
            preferred_element_type=jnp.float32,
        )
        store(g2, hg2, start, n2, factor * (1.0 - t * t))

    def weight_grad(layer, g_ref, x_ref, h_ref, step):
        wacc[...] = jnp.zeros_like(wacc)

        @pl.loop(0, sub // n4)
        def _(block):
            start = HALO + block * n4
            wacc[...] += lax.dot_general(
                g_ref[pl.ds(start, n4)].reshape(n4 * groups, lanes),
                taps(x_ref, h_ref, start, n4, step),
                (((0,), (0,)), ((), ())),
                preferred_element_type=jnp.float32,
            )

        out_diag = lax.shift_right_logical(
            lax.broadcasted_iota(jnp.int32, (lanes, width), 0), 5
        )
        in_diag = diag_of(
            lax.shift_right_logical(lax.broadcasted_iota(jnp.int32, (lanes, width), 1), 5)
        )
        fold = (
            lax.broadcasted_iota(jnp.int32, (width, 32), 0) & 31
            == lax.broadcasted_iota(jnp.int32, (width, 32), 1)
        ).astype(jnp.float32)
        for a in range(3):
            product = wacc[:, a * width : (a + 1) * width]
            for b in range(3):
                picked = jnp.where(in_diag == out_diag + (b - 1) * step, product, 0.0)
                total_rows = picked[:32]
                for d in range(1, PACK):
                    total_rows = total_rows + picked[32 * d : 32 * (d + 1)]
                wgrad[layer, 3 * a + b] = jnp.dot(
                    total_rows, fold, precision=HIGHEST, preferred_element_type=jnp.float32
                )

    weight_grad(1, g2, x1, h1, dil_two)

    @pl.loop(0, (sub + 2 * MAXDIL) // n3)
    def _(block):
        start = 3 * MAXDIL + block * n3
        back = conv(g2, hg2, 2, start, n3, dil_two)
        b1[pl.ds(start, n3)] = back.reshape(n3, groups, lanes)
        scale = s1[pl.ds(start, n3)].reshape(n3 * groups, lanes).astype(jnp.float32)
        store(x1, h1, start, n3, back * scale)

    weight_grad(0, x1, x0, h0, dil_one)
    grad_right[...] = jnp.zeros_like(grad_right)

    @pl.loop(0, sub // n4)
    def _(block):
        start = HALO + block * n4
        back = conv(x1, h1, 3, start, n4, dil_one)
        scale = s0[pl.ds(start, n4)].reshape(n4 * groups, lanes).astype(jnp.float32)
        grad = (back + b1[pl.ds(start, n4)].reshape(n4 * groups, lanes)) * scale
        grad_left[block] = jnp.sum(grad.reshape(n4, groups, lanes), axis=1)
        for u in range(n4):
            at = pl.ds(block * n4 + u, groups, stride=PACK)
            for half in range(2):
                piece = grad[u * groups : (u + 1) * groups, 128 * half : 128 * (half + 1)]
                grad_right[half, at, :] = grad_right[half, at, :] + piece


def swapped(me, bit):
    return me + bit - 2 * bit * ((me // bit) % 2)


def tail(
    plan, both_in, conv_in, embeddings, projection, embed_out, proj_out, conv_out,
    both, both_slots, conv, conv_slots, spill_slot, sums, sum_slots, send, recv,
):
    n_bin, n_diag, rows, scaling = plan
    me_bin, me_diag = lax.axis_index("bin"), lax.axis_index("diag")
    diag_bits = [1 << k for k in range(n_diag.bit_length() - 1)]
    bin_bits = [1 << k for k in range(n_bin.bit_length() - 1)]
    after = {"bin": (me_bin + 1) % n_bin}
    before = {"bin": (me_bin + n_bin - 1) % n_bin}
    partners = [{"diag": swapped(me_diag, bit)} for bit in diag_bits]
    partners += [{"bin": swapped(me_bin, bit)} for bit in bin_bits]
    barrier = pltpu.get_barrier_semaphore()
    for partner in partners + [after, before]:
        pl.semaphore_signal(
            barrier, inc=1, device_id=partner, device_id_type=pl.DeviceIdType.MESH
        )
    pl.semaphore_wait(barrier, len(partners) + 2)

    def copy(source, target, at, device):
        return pltpu.make_async_remote_copy(
            src_ref=source, dst_ref=target, send_sem=send.at[at], recv_sem=recv.at[at],
            device_id=device, device_id_type=pl.DeviceIdType.MESH,
        )

    both[...] = both_in[...]
    conv[...] = conv_in[...]
    for k in range(len(diag_bits)):
        first = copy(both, both_slots.at[k], 2 * k, partners[k])
        second = copy(conv, conv_slots.at[k], 2 * k + 1, partners[k])
        first.start()
        second.start()
        first.wait()
        both[...] += both_slots[k]
        second.wait()
        conv[...] += conv_slots[k]
    at = 2 * len(diag_bits)
    half = both.shape[0] // 2
    spill = both.shape[1] - rows
    hop = copy(both.at[pl.ds(half, half), pl.ds(rows, spill)], spill_slot, at, after)
    hop.start()
    hop.wait()
    both[half:, :spill] += spill_slot[...]
    summed = both[:, :rows]
    part = lax.dot_general(
        summed, embeddings[...].astype(jnp.float32), (((1,), (1,)), ((), ())),
        precision=HIGHEST, preferred_element_type=jnp.float32,
    )
    count = conv.shape[0]
    sums[:count] = conv[...]
    sums[count:] = jnp.zeros_like(sums[count:])
    sums[count:, : part.shape[1]] = part
    for k in range(len(bin_bits)):
        step = copy(sums, sum_slots.at[k], at + 1 + k, partners[len(diag_bits) + k])
        step.start()
        if k == 0:
            embed_out[...] = lax.dot_general(
                projection[...].astype(jnp.float32), summed, (((1,), (0,)), ((), ())),
                precision=HIGHEST, preferred_element_type=jnp.float32,
            )
        step.wait()
        sums[...] += sum_slots[k]
    conv_out[...] = sums[:count] * scaling
    proj_out[...] = sums[count:, : part.shape[1]] * scaling


def split_two(x):
    high = x.astype(jnp.bfloat16)
    return high, (x - high.astype(jnp.float32)).astype(jnp.bfloat16)


def shifted(axis, size, by):
    return [(i, i + by) for i in range(size) if 0 <= i + by < size]


def on_device(
    embeddings, projection, dist_bias, conv_weight, head_weight, dilations, band_limit, cotangent
):
    channels = conv_weight.shape[2]
    diag_dev, rows_dev = cotangent.shape
    n_bin, n_diag = lax.axis_size("bin"), lax.axis_size("diag")
    total_bins, diags = rows_dev * n_bin, diag_dev * n_diag
    me = lax.axis_index("diag")
    first_row = lax.axis_index("bin") * rows_dev
    sub = rows_dev // n_diag
    groups = diags // PACK
    lanes = PACK * channels
    reach = HALO + diags

    def around(block, before, after):
        low = lax.ppermute(block[:, rows_dev - before :], "bin", shifted("bin", n_bin, 1))
        high = lax.ppermute(block[:, :after], "bin", shifted("bin", n_bin, -1))
        return jnp.concatenate([low, block, high], axis=1)

    def pairs(k):
        return [(i, (i + k) % n_diag) for i in range(n_diag)]

    wide = around(embeddings, HALO, reach)
    part = jnp.einsum("eb,ek->bk", wide, projection, preferred_element_type=jnp.float32)
    span = sub + HALO + reach
    projected = lax.dynamic_slice_in_dim(part, me * sub, span, 0)
    for k in range(1, n_diag):
        other = lax.rem(me + k, n_diag)
        projected = projected + lax.ppermute(
            lax.dynamic_slice_in_dim(part, other * sub, span, 0), "diag", pairs(k)
        )
    region = sub + 2 * HALO
    reads = region + PACK * (groups - 1)
    left = jnp.tile(projected[:region, :channels], (1, PACK))
    right = jnp.concatenate(
        [projected[d : d + reads, channels:] for d in range(PACK)], axis=1
    )
    halves = lambda x: jnp.stack([x[:, : lanes // 2], x[:, lanes // 2 :]])
    bias = jnp.transpose(dist_bias.reshape(channels, groups, PACK), (1, 2, 0)).reshape(
        groups, lanes
    )

    row_ids = first_row + jnp.arange(rows_dev, dtype=jnp.int32)[None, :]
    diag_ids = me * diag_dev + jnp.arange(diag_dev, dtype=jnp.int32)[:, None]
    counted = (row_ids + diag_ids < total_bins) & (diag_ids < band_limit[None, :])
    margin = 2 * MAXDIL
    cot_wide = around(jnp.where(counted, cotangent, 0.0), margin, margin)
    cot_span = sub + 2 * margin
    cot = jnp.zeros((n_diag, diag_dev, cot_span), jnp.float32)
    for k in range(n_diag):
        other = lax.rem(me + k, n_diag)
        piece = lax.dynamic_slice_in_dim(cot_wide, other * sub, cot_span, 1)
        if k:
            piece = lax.ppermute(piece, "diag", pairs(k))
        cot = lax.dynamic_update_index_in_dim(cot, piece, lax.rem(me - k + n_diag, n_diag), 0)
    n1 = cut(sub + 6 * MAXDIL, 24)
    n2 = cut(cot_span, 16)
    n3 = cut(sub + 2 * MAXDIL, 25)
    n4 = cut(sub, 24)
    blocks = cot_span // n2
    cot = jnp.transpose(cot.reshape(groups, PACK, blocks, n2), (2, 1, 3, 0)).reshape(
        blocks, PACK, n2 * groups
    )
    cot_high, cot_low = split_two(cot)
    head_high, head_low = split_two(head_weight)
    eye = jnp.eye(PACK, dtype=jnp.bfloat16)
    spread = lambda h: (eye[:, :, None] * h[None, None, :]).reshape(PACK, lanes)
    pad = jnp.zeros((PACK, lanes), jnp.bfloat16)
    cots = jnp.concatenate([cot_high, cot_low, cot_high, jnp.zeros_like(cot_high)], axis=1)
    expand = jnp.concatenate([spread(head_high), spread(head_high), spread(head_low), pad])
    head = jnp.concatenate([spread(head_high), spread(head_low)])
    info = jnp.concatenate([dilations, (first_row + me * sub - HALO)[None].astype(jnp.int32)])

    writes = sub + PACK * (groups - 1)
    vmem = pl.BlockSpec(memory_space=pltpu.VMEM)
    half_map = pltpu.VMEM((region, groups, lanes), jnp.bfloat16)
    pred, grad_left, grad_right, conv_part = pl.pallas_call(
        functools.partial(kernel, (sub, groups, total_bins, n1, n2, n3, n4)),
        out_shape=[
            jax.ShapeDtypeStruct((blocks, PACK, n2 * groups), jnp.float32),
            jax.ShapeDtypeStruct((sub // n4, n4, lanes), jnp.float32),
            jax.ShapeDtypeStruct((2, writes, lanes // 2), jnp.float32),
            jax.ShapeDtypeStruct(conv_weight.shape, jnp.float32),
        ],
        in_specs=[pl.BlockSpec(memory_space=pltpu.SMEM)] + [vmem] * 7,
        out_specs=[vmem] * 4,
        scratch_shapes=[half_map] * 8
        + [
            pltpu.VMEM((region, groups, lanes), jnp.float32),
            pltpu.VMEM((lanes, 6 * lanes), jnp.float32),
            pltpu.VMEM((4, 6 * lanes, lanes), jnp.bfloat16),
        ],
        compiler_params=pltpu.CompilerParams(vmem_limit_bytes=60 * 1024 * 1024),
        name="band",
    )(info, halves(left), halves(right), bias, conv_weight, expand, head, cots)

    grad_right = jnp.concatenate([grad_right[0], grad_right[1]], axis=1)
    spilled = jnp.zeros((sub + diags, channels), jnp.float32)
    for d in range(PACK):
        spilled = spilled + jnp.pad(
            grad_right[:, d * channels : (d + 1) * channels],
            ((d, sub + diags - writes - d), (0, 0)),
        )
    lefts = jnp.sum(grad_left.reshape(sub, PACK, channels), axis=1)
    own = jnp.concatenate([jnp.pad(lefts, ((0, diags), (0, 0))), spilled], axis=1)
    buffer = lax.dynamic_update_slice_in_dim(
        jnp.zeros((rows_dev + diags, 2 * channels), jnp.float32), own, me * sub, 0
    )
    conv_rows = conv_part.size // 128
    features = embeddings.shape[0]
    scaling = 1.0 / math.sqrt(total_bins * diags)
    wide_both = (2 * channels, rows_dev + diags)
    diag_steps, bin_steps = n_diag.bit_length() - 1, n_bin.bit_length() - 1
    sum_rows = conv_rows + 2 * channels
    grad_embed, proj_sum, conv_sum = pl.pallas_call(
        functools.partial(tail, (n_bin, n_diag, rows_dev, scaling)),
        out_shape=[
            jax.ShapeDtypeStruct((features, rows_dev), jnp.float32),
            jax.ShapeDtypeStruct((2 * channels, features), jnp.float32),
            jax.ShapeDtypeStruct((conv_rows, 128), jnp.float32),
        ],
        in_specs=[vmem] * 4,
        out_specs=[vmem] * 3,
        scratch_shapes=[
            pltpu.VMEM(wide_both, jnp.float32),
            pltpu.VMEM((diag_steps,) + wide_both, jnp.float32),
            pltpu.VMEM((conv_rows, 128), jnp.float32),
            pltpu.VMEM((diag_steps, conv_rows, 128), jnp.float32),
            pltpu.VMEM((channels, diags), jnp.float32),
            pltpu.VMEM((sum_rows, 128), jnp.float32),
            pltpu.VMEM((bin_steps, sum_rows, 128), jnp.float32),
            pltpu.SemaphoreType.DMA((2 * diag_steps + 1 + bin_steps,)),
            pltpu.SemaphoreType.DMA((2 * diag_steps + 1 + bin_steps,)),
        ],
        compiler_params=pltpu.CompilerParams(collective_id=0, has_side_effects=True),
        name="tail",
    )(jnp.transpose(buffer), conv_part.reshape(conv_rows, 128), embeddings, projection)
    grad_proj = jnp.transpose(proj_sum)
    grad_conv = conv_sum.reshape(conv_part.shape)

    pred = jnp.transpose(pred.reshape(blocks, PACK, n2, groups), (3, 1, 0, 2)).reshape(
        diags, cot_span
    )[:, margin : margin + sub]
    pred_local = jnp.zeros((diag_dev, rows_dev), jnp.float32)
    for k in range(n_diag):
        other = lax.rem(me + k, n_diag)
        piece = lax.dynamic_slice_in_dim(pred, other * diag_dev, diag_dev, 0)
        if k:
            piece = lax.ppermute(piece, "diag", pairs(k))
        pred_local = lax.dynamic_update_slice_in_dim(
            pred_local, piece, lax.rem(me - k + n_diag, n_diag) * sub, 1
        )
    pred_local = jnp.where(counted, pred_local, 0.0)
    return (pred_local, grad_embed, grad_proj, grad_conv)


def solution(mesh):
    return jax.shard_map(
        on_device,
        mesh=mesh,
        in_specs=(
            P("diag", "bin"),
            P("diag", None),
            P(),
            P(),
            P(),
            P(),
            P("bin"),
            P("diag", "bin"),
        ),
        out_specs=(P("diag", "bin"), P("diag", "bin"), P("diag", None), P()),
        check_vma=False,
    )
```

```python
import functools
import math

import jax
import jax.numpy as jnp
from jax import lax
from jax.experimental import pallas as pl
from jax.experimental.pallas import tpu as pltpu
from jax.sharding import PartitionSpec as P

MAXDIL = 4
HALO = 4 * MAXDIL
PACK = 8


HIGHEST = lax.Precision.HIGHEST


def cut(rows, most):
    return max(n for n in range(1, most + 1) if rows % n == 0)


def steps(blocks):
    many = 2 if blocks % 2 == 0 else 3 if blocks % 3 == 0 else 1

    def run(body):
        @pl.loop(0, blocks // many)
        def _(turn):
            for u in range(many):
                body(turn * many + u)

    return run


def kernel(
    plan, info, left, right, bias, weights, expand, head, cots, pred, grad_left, grad_right,
    wgrad, x0, h0, s0, x1, h1, s1, g2, hg2, b1, wacc, mats,
):
    sub, groups, total, n1, n2, n3, n4 = plan
    lanes = 256
    first = info[2]
    dil_one, dil_two = info[0], info[1]
    g_ids = lax.broadcasted_iota(jnp.int32, (groups, lanes), 0)
    diag_ids = g_ids * PACK + lax.shift_right_logical(
        lax.broadcasted_iota(jnp.int32, (groups, lanes), 1), 5
    )

    def inside_rows(start, count):
        rows = first + start + lax.broadcasted_iota(jnp.int32, (count, 1, 1), 0)
        bound = jnp.where(rows >= 0, total - rows, 0)
        return (diag_ids[None] < bound).reshape(count * groups, lanes)

    def store(x_ref, h_ref, start, count, value):
        value = value.astype(jnp.bfloat16).astype(jnp.float32)
        x_ref[pl.ds(start, count)] = value.astype(jnp.bfloat16).reshape(count, groups, lanes)
        size = count * groups
        g_row = lax.broadcasted_iota(jnp.int32, (count, groups, 128), 1).reshape(size, 128)
        below = jnp.where(g_row == 0, 0.0, pltpu.roll(value[:, 128:], 1, 0))
        above = jnp.where(g_row == groups - 1, 0.0, pltpu.roll(value[:, :128], size - 1, 0))
        h_ref[pl.ds(start, count), :, :128] = below.astype(jnp.bfloat16).reshape(
            count, groups, 128
        )
        h_ref[pl.ds(start, count), :, 128:] = above.astype(jnp.bfloat16).reshape(
            count, groups, 128
        )

    def taps(x_ref, h_ref, start, count, step):
        pieces = []
        for along in (-1, 0, 1):
            at = start + along * step
            pieces.append(x_ref[pl.ds(at, count)].reshape(count * groups, lanes))
            pieces.append(h_ref[pl.ds(at, count)].reshape(count * groups, lanes))
        return jnp.concatenate(pieces, axis=1)

    def conv(x_ref, h_ref, mat, start, count, step):
        return jnp.dot(
            taps(x_ref, h_ref, start, count, step),
            mats[mat],
            preferred_element_type=jnp.float32,
        )

    width = 2 * lanes

    def diag_of(slot):
        return jnp.where(slot < 8, slot, jnp.where(slot < 12, slot - 12, slot - 4))

    delta = diag_of(
        lax.shift_right_logical(lax.broadcasted_iota(jnp.int32, (width, lanes), 0), 5)
    ) - lax.shift_right_logical(lax.broadcasted_iota(jnp.int32, (width, lanes), 1), 5)
    repeat = (
        lax.broadcasted_iota(jnp.int32, (32, lanes), 0)
        == lax.broadcasted_iota(jnp.int32, (32, lanes), 1) & 31
    ).astype(jnp.bfloat16)
    for mat, layer, sign, step in (
        (0, 0, 1, dil_one), (1, 1, 1, dil_two), (2, 1, -1, dil_two), (3, 0, -1, dil_one)
    ):
        for along in range(3):
            taken = along if sign > 0 else 2 - along
            total_mat = jnp.zeros((width, lanes), jnp.float32)
            for b in range(3):
                spread = lax.dot_general(
                    weights[layer, 3 * taken + b], repeat,
                    (((0 if sign > 0 else 1,), (0,)), ((), ())),
                    preferred_element_type=jnp.float32,
                )
                total_mat = jnp.where(
                    delta == sign * (b - 1) * step,
                    jnp.concatenate([spread] * 16, axis=0),
                    total_mat,
                )
            mats[mat, along * width : (along + 1) * width] = total_mat.astype(jnp.bfloat16)

    n0 = 4

    @steps((sub + 2 * HALO) // n0)
    def _(block):
        start = block * n0
        rows = []
        for u in range(n0):
            at = start + u
            halves = []
            for half in range(2):
                partner = right[half, pl.ds(at, groups, stride=PACK), :]
                halves.append(partner + left[half, pl.ds(at, 1), :])
            rows.append(jnp.concatenate(halves, axis=1) + bias[...])
        t = jnp.tanh(jnp.concatenate(rows, axis=0))
        keep = inside_rows(start, n0)
        s0[pl.ds(start, n0)] = (
            jnp.where(keep, 1.0 - t * t, 0.0).reshape(n0, groups, lanes)
        )
        store(x0, h0, start, n0, jnp.where(keep, t, 0.0))

    @steps((sub + 6 * MAXDIL) // n1)
    def _(block):
        start = MAXDIL + block * n1
        t = jnp.tanh(conv(x0, h0, 0, start, n1, dil_one))
        keep = inside_rows(start, n1)
        s1[pl.ds(start, n1)] = (
            jnp.where(keep, 1.0 - t * t, 0.0).reshape(n1, groups, lanes)
        )
        before = x0[pl.ds(start, n1)].reshape(n1 * groups, lanes).astype(jnp.float32)
        store(x1, h1, start, n1, jnp.where(keep, before + t, 0.0))

    @steps((sub + 4 * MAXDIL) // n2)
    def _(block):
        start = 2 * MAXDIL + block * n2
        t = jnp.tanh(conv(x1, h1, 1, start, n2, dil_two))
        t_high = t.astype(jnp.bfloat16)
        t_low = (t - t_high.astype(jnp.float32)).astype(jnp.bfloat16)
        scored = lax.dot_general(
            head[...], t_high, (((1,), (1,)), ((), ())), preferred_element_type=jnp.float32
        ) + lax.dot_general(
            head[...], t_low, (((1,), (1,)), ((), ())), preferred_element_type=jnp.float32
        )
        pred[block] = scored[:PACK] + scored[PACK:]
        factor = lax.dot_general(
            cots[block], expand[...], (((0,), (0,)), ((), ())),
            preferred_element_type=jnp.float32,
        )
        store(g2, hg2, start, n2, factor * (1.0 - t * t))

    def weight_grad(layer, g_ref, x_ref, h_ref, step):
        wacc[...] = jnp.zeros_like(wacc)

        @steps(sub // n4)
        def _(block):
            start = HALO + block * n4
            wacc[...] += lax.dot_general(
                g_ref[pl.ds(start, n4)].reshape(n4 * groups, lanes),
                taps(x_ref, h_ref, start, n4, step),
                (((0,), (0,)), ((), ())),
                preferred_element_type=jnp.float32,
            )

        out_diag = lax.shift_right_logical(
            lax.broadcasted_iota(jnp.int32, (lanes, width), 0), 5
        )
        in_diag = diag_of(
            lax.shift_right_logical(lax.broadcasted_iota(jnp.int32, (lanes, width), 1), 5)
        )
        fold = (
            lax.broadcasted_iota(jnp.int32, (width, 32), 0) & 31
            == lax.broadcasted_iota(jnp.int32, (width, 32), 1)
        ).astype(jnp.float32)
        for a in range(3):
            product = wacc[:, a * width : (a + 1) * width]
            for b in range(3):
                picked = jnp.where(in_diag == out_diag + (b - 1) * step, product, 0.0)
                total_rows = picked[:32]
                for d in range(1, PACK):
                    total_rows = total_rows + picked[32 * d : 32 * (d + 1)]
                wgrad[layer, 3 * a + b] = jnp.dot(
                    total_rows, fold, precision=HIGHEST, preferred_element_type=jnp.float32
                )

    weight_grad(1, g2, x1, h1, dil_two)

    @steps((sub + 2 * MAXDIL) // n3)
    def _(block):
        start = 3 * MAXDIL + block * n3
        back = conv(g2, hg2, 2, start, n3, dil_two)
        b1[pl.ds(start, n3)] = back.reshape(n3, groups, lanes)
        scale = s1[pl.ds(start, n3)].reshape(n3 * groups, lanes)
        store(x1, h1, start, n3, back * scale)

    weight_grad(0, x1, x0, h0, dil_one)
    grad_right[...] = jnp.zeros_like(grad_right)

    @steps(sub // n4)
    def _(block):
        start = HALO + block * n4
        back = conv(x1, h1, 3, start, n4, dil_one)
        scale = s0[pl.ds(start, n4)].reshape(n4 * groups, lanes)
        grad = (back + b1[pl.ds(start, n4)].reshape(n4 * groups, lanes)) * scale
        grad_left[block] = jnp.sum(grad.reshape(n4, groups, lanes), axis=1)
        for u in range(n4):
            at = pl.ds(block * n4 + u, groups, stride=PACK)
            for half in range(2):
                piece = grad[u * groups : (u + 1) * groups, 128 * half : 128 * (half + 1)]
                grad_right[half, at, :] = grad_right[half, at, :] + piece


def swapped(me, bit):
    return me + bit - 2 * bit * ((me // bit) % 2)


def tail(
    plan, both_in, conv_in, embeddings, projection, embed_out, proj_out, conv_out,
    both, both_slots, conv_slots, spill_slot, sums, cut_slot, held, sum_slots, far_slot,
    send, recv,
):
    n_bin, n_diag, rows, scaling = plan
    me_bin, me_diag = lax.axis_index("bin"), lax.axis_index("diag")
    diag_bits = [1 << k for k in range(n_diag.bit_length() - 1)]
    bin_bits = [1 << k for k in range(n_bin.bit_length() - 1)]
    after = {"bin": (me_bin + 1) % n_bin}
    before = {"bin": (me_bin + n_bin - 1) % n_bin}
    partners = [{"diag": swapped(me_diag, bit)} for bit in diag_bits]
    partners += [{"bin": swapped(me_bin, bit)} for bit in bin_bits]
    barrier = pltpu.get_barrier_semaphore()
    for partner in partners + [after, before]:
        pl.semaphore_signal(
            barrier, inc=1, device_id=partner, device_id_type=pl.DeviceIdType.MESH
        )
    pl.semaphore_wait(barrier, len(partners) + 2)

    near = partners[len(diag_bits)]
    ids = iter(range(64))
    count, half = conv_in.shape[0], both.shape[0] // 2

    def copy(source, target, at, device):
        return pltpu.make_async_remote_copy(
            src_ref=source, dst_ref=target, send_sem=send.at[at], recv_sem=recv.at[at],
            device_id=device, device_id_type=pl.DeviceIdType.MESH,
        )

    both[...] = both_in[...]
    sums[:count] = conv_in[...]
    mine, theirs = me_bin % 2, 1 - me_bin % 2
    conv_half, proj_half = count // 2, half

    def exchange(rows_at, size, slot, device):
        return copy(sums.at[pl.ds(rows_at, size)], slot, next(ids), device)

    conv_cut = exchange(theirs * conv_half, conv_half, cut_slot.at[pl.ds(0, conv_half)], near)
    conv_cut.start()
    for k in range(len(diag_bits)):
        first = copy(both, both_slots.at[k], next(ids), partners[k])
        first.start()
        first.wait()
        both[...] += both_slots[k]
    conv_cut.wait()
    held[:conv_half] = sums[pl.ds(mine * conv_half, conv_half)] + cut_slot[:conv_half]
    spill = both.shape[1] - rows
    hop = copy(both.at[pl.ds(half, half), pl.ds(rows, spill)], spill_slot, next(ids), after)
    hop.start()
    for k in range(len(diag_bits)):
        second = copy(
            held.at[pl.ds(0, conv_half)], conv_slots.at[k], next(ids), partners[k]
        )
        second.start()
        second.wait()
        held[:conv_half] += conv_slots[k]
    hop.wait()
    both[half:, :spill] += spill_slot[...]
    summed = both[:, :rows]
    part = lax.dot_general(
        summed, embeddings[...].astype(jnp.float32), (((1,), (1,)), ((), ())),
        precision=HIGHEST, preferred_element_type=jnp.float32,
    )
    features = part.shape[1]
    sums[count:] = jnp.zeros_like(sums[count:])
    sums[count:, :features] = part
    proj_cut = exchange(
        count + theirs * proj_half, proj_half, cut_slot.at[pl.ds(conv_half, proj_half)], near
    )
    proj_cut.start()
    embed_out[...] = lax.dot_general(
        projection[...].astype(jnp.float32), summed, (((1,), (0,)), ((), ())),
        precision=HIGHEST, preferred_element_type=jnp.float32,
    )
    proj_cut.wait()
    held[conv_half:] = (
        sums[pl.ds(count + mine * proj_half, proj_half)] + cut_slot[conv_half:]
    )
    for k in range(1, len(bin_bits)):
        step = copy(held, sum_slots.at[k - 1], next(ids), partners[len(diag_bits) + k])
        step.start()
        step.wait()
        held[...] += sum_slots[k - 1]
    last = copy(held, far_slot, next(ids), near)
    last.start()
    last.wait()
    own, far = held[...] * scaling, far_slot[...] * scaling
    conv_out[pl.ds(mine * conv_half, conv_half)] = own[:conv_half]
    conv_out[pl.ds(theirs * conv_half, conv_half)] = far[:conv_half]
    proj_out[pl.ds(mine * proj_half, proj_half)] = own[conv_half:, :features]
    proj_out[pl.ds(theirs * proj_half, proj_half)] = far[conv_half:, :features]


def split_two(x):
    high = x.astype(jnp.bfloat16)
    return high, (x - high.astype(jnp.float32)).astype(jnp.bfloat16)


def shifted(axis, size, by):
    return [(i, i + by) for i in range(size) if 0 <= i + by < size]


def on_device(
    embeddings, projection, dist_bias, conv_weight, head_weight, dilations, band_limit, cotangent
):
    channels = conv_weight.shape[2]
    diag_dev, rows_dev = cotangent.shape
    n_bin, n_diag = lax.axis_size("bin"), lax.axis_size("diag")
    total_bins, diags = rows_dev * n_bin, diag_dev * n_diag
    me = lax.axis_index("diag")
    first_row = lax.axis_index("bin") * rows_dev
    sub = rows_dev // n_diag
    groups = diags // PACK
    lanes = PACK * channels
    reach = HALO + diags

    def around(block, before, after):
        low = lax.ppermute(block[:, rows_dev - before :], "bin", shifted("bin", n_bin, 1))
        high = lax.ppermute(block[:, :after], "bin", shifted("bin", n_bin, -1))
        return jnp.concatenate([low, block, high], axis=1)

    def pairs(k):
        return [(i, (i + k) % n_diag) for i in range(n_diag)]

    wide = around(embeddings, HALO, reach)
    part = jnp.einsum("eb,ek->bk", wide, projection, preferred_element_type=jnp.float32)
    span = sub + HALO + reach
    projected = lax.dynamic_slice_in_dim(part, me * sub, span, 0)
    for k in range(1, n_diag):
        other = lax.rem(me + k, n_diag)
        projected = projected + lax.ppermute(
            lax.dynamic_slice_in_dim(part, other * sub, span, 0), "diag", pairs(k)
        )
    region = sub + 2 * HALO
    reads = region + PACK * (groups - 1)
    left = jnp.tile(projected[:region, :channels], (1, PACK))
    right = jnp.concatenate(
        [projected[d : d + reads, channels:] for d in range(PACK)], axis=1
    )
    halves = lambda x: jnp.stack([x[:, : lanes // 2], x[:, lanes // 2 :]])
    bias = jnp.transpose(dist_bias.reshape(channels, groups, PACK), (1, 2, 0)).reshape(
        groups, lanes
    )

    row_ids = first_row + jnp.arange(rows_dev, dtype=jnp.int32)[None, :]
    diag_ids = me * diag_dev + jnp.arange(diag_dev, dtype=jnp.int32)[:, None]
    counted = (row_ids + diag_ids < total_bins) & (diag_ids < band_limit[None, :])
    margin = 2 * MAXDIL
    cot_wide = around(jnp.where(counted, cotangent, 0.0), margin, margin)
    cot_span = sub + 2 * margin
    cot = jnp.zeros((n_diag, diag_dev, cot_span), jnp.float32)
    for k in range(n_diag):
        other = lax.rem(me + k, n_diag)
        piece = lax.dynamic_slice_in_dim(cot_wide, other * sub, cot_span, 1)
        if k:
            piece = lax.ppermute(piece, "diag", pairs(k))
        cot = lax.dynamic_update_index_in_dim(cot, piece, lax.rem(me - k + n_diag, n_diag), 0)
    n1 = cut(sub + 6 * MAXDIL, 12)
    n2 = cut(cot_span, 8)
    n3 = cut(sub + 2 * MAXDIL, 10)
    n4 = cut(sub, 16)
    blocks = cot_span // n2
    cot = jnp.transpose(cot.reshape(groups, PACK, blocks, n2), (2, 1, 3, 0)).reshape(
        blocks, PACK, n2 * groups
    )
    cot_high, cot_low = split_two(cot)
    head_high, head_low = split_two(head_weight)
    eye = jnp.eye(PACK, dtype=jnp.bfloat16)
    spread = lambda h: (eye[:, :, None] * h[None, None, :]).reshape(PACK, lanes)
    pad = jnp.zeros((PACK, lanes), jnp.bfloat16)
    cots = jnp.concatenate([cot_high, cot_low, cot_high, jnp.zeros_like(cot_high)], axis=1)
    expand = jnp.concatenate([spread(head_high), spread(head_high), spread(head_low), pad])
    head = jnp.concatenate([spread(head_high), spread(head_low)])
    info = jnp.concatenate([dilations, (first_row + me * sub - HALO)[None].astype(jnp.int32)])

    writes = sub + PACK * (groups - 1)
    vmem = pl.BlockSpec(memory_space=pltpu.VMEM)
    full_map = pltpu.VMEM((region, groups, lanes), jnp.float32)
    half_map = pltpu.VMEM((region, groups, lanes), jnp.bfloat16)
    pred, grad_left, grad_right, conv_part = pl.pallas_call(
        functools.partial(kernel, (sub, groups, total_bins, n1, n2, n3, n4)),
        out_shape=[
            jax.ShapeDtypeStruct((blocks, PACK, n2 * groups), jnp.float32),
            jax.ShapeDtypeStruct((sub // n4, n4, lanes), jnp.float32),
            jax.ShapeDtypeStruct((2, writes, lanes // 2), jnp.float32),
            jax.ShapeDtypeStruct(conv_weight.shape, jnp.float32),
        ],
        in_specs=[pl.BlockSpec(memory_space=pltpu.SMEM)] + [vmem] * 7,
        out_specs=[vmem] * 4,
        scratch_shapes=[half_map] * 2
        + [full_map]
        + [half_map] * 2
        + [full_map]
        + [half_map] * 2
        + [
            full_map,
            pltpu.VMEM((lanes, 6 * lanes), jnp.float32),
            pltpu.VMEM((4, 6 * lanes, lanes), jnp.bfloat16),
        ],
        compiler_params=pltpu.CompilerParams(vmem_limit_bytes=60 * 1024 * 1024),
        name="band",
    )(info, halves(left), halves(right), bias, conv_weight, expand, head, cots)

    grad_right = jnp.concatenate([grad_right[0], grad_right[1]], axis=1)
    spilled = jnp.zeros((sub + diags, channels), jnp.float32)
    for d in range(PACK):
        spilled = spilled + jnp.pad(
            grad_right[:, d * channels : (d + 1) * channels],
            ((d, sub + diags - writes - d), (0, 0)),
        )
    lefts = jnp.sum(grad_left.reshape(sub, PACK, channels), axis=1)
    own = jnp.concatenate([jnp.pad(lefts, ((0, diags), (0, 0))), spilled], axis=1)
    buffer = lax.dynamic_update_slice_in_dim(
        jnp.zeros((rows_dev + diags, 2 * channels), jnp.float32), own, me * sub, 0
    )
    conv_rows = conv_part.size // 128
    features = embeddings.shape[0]
    scaling = 1.0 / math.sqrt(total_bins * diags)
    wide_both = (2 * channels, rows_dev + diags)
    diag_steps, bin_steps = n_diag.bit_length() - 1, n_bin.bit_length() - 1
    sum_rows = conv_rows + 2 * channels
    grad_embed, proj_sum, conv_sum = pl.pallas_call(
        functools.partial(tail, (n_bin, n_diag, rows_dev, scaling)),
        out_shape=[
            jax.ShapeDtypeStruct((features, rows_dev), jnp.float32),
            jax.ShapeDtypeStruct((2 * channels, features), jnp.float32),
            jax.ShapeDtypeStruct((conv_rows, 128), jnp.float32),
        ],
        in_specs=[vmem] * 4,
        out_specs=[vmem] * 3,
        scratch_shapes=[
            pltpu.VMEM(wide_both, jnp.float32),
            pltpu.VMEM((diag_steps,) + wide_both, jnp.float32),
            pltpu.VMEM((diag_steps, conv_rows // 2, 128), jnp.float32),
            pltpu.VMEM((channels, diags), jnp.float32),
            pltpu.VMEM((sum_rows, 128), jnp.float32),
            pltpu.VMEM((sum_rows // 2, 128), jnp.float32),
            pltpu.VMEM((sum_rows // 2, 128), jnp.float32),
            pltpu.VMEM((bin_steps - 1, sum_rows // 2, 128), jnp.float32),
            pltpu.VMEM((sum_rows // 2, 128), jnp.float32),
            pltpu.SemaphoreType.DMA((2 * diag_steps + bin_steps + 3,)),
            pltpu.SemaphoreType.DMA((2 * diag_steps + bin_steps + 3,)),
        ],
        compiler_params=pltpu.CompilerParams(collective_id=0, has_side_effects=True),
        name="tail",
    )(jnp.transpose(buffer), conv_part.reshape(conv_rows, 128), embeddings, projection)
    grad_proj = jnp.transpose(proj_sum)
    grad_conv = conv_sum.reshape(conv_part.shape)

    pred = jnp.transpose(pred.reshape(blocks, PACK, n2, groups), (3, 1, 0, 2)).reshape(
        diags, cot_span
    )[:, margin : margin + sub]
    pred_local = jnp.zeros((diag_dev, rows_dev), jnp.float32)
    for k in range(n_diag):
        other = lax.rem(me + k, n_diag)
        piece = lax.dynamic_slice_in_dim(pred, other * diag_dev, diag_dev, 0)
        if k:
            piece = lax.ppermute(piece, "diag", pairs(k))
        pred_local = lax.dynamic_update_slice_in_dim(
            pred_local, piece, lax.rem(me - k + n_diag, n_diag) * sub, 1
        )
    pred_local = jnp.where(counted, pred_local, 0.0)
    return (pred_local, grad_embed, grad_proj, grad_conv)


def solution(mesh):
    return jax.shard_map(
        on_device,
        mesh=mesh,
        in_specs=(
            P("diag", "bin"),
            P("diag", None),
            P(),
            P(),
            P(),
            P(),
            P("bin"),
            P("diag", "bin"),
        ),
        out_specs=(P("diag", "bin"), P("diag", "bin"), P("diag", None), P()),
        check_vma=False,
    )
```

```python
import functools
import math

import jax
import jax.numpy as jnp
from jax import lax
from jax.experimental import pallas as pl
from jax.experimental.pallas import tpu as pltpu
from jax.sharding import PartitionSpec as P

MAXDIL = 4
HALO = 4 * MAXDIL
PACK = 8


HIGHEST = lax.Precision.HIGHEST


def cut(rows, most):
    return max(n for n in range(1, most + 1) if rows % n == 0)


def kernel(
    plan, info, left, right, bias, weights, expand, head, cots, pred, grad_left, grad_right,
    wgrad, x0, h0, s0, x1, h1, s1, g2, hg2, b1, wacc, mats,
):
    sub, groups, total, n1, n2, n3, n4 = plan
    lanes = 256
    first = info[2]
    dil_one, dil_two = info[0], info[1]
    g_ids = lax.broadcasted_iota(jnp.int32, (groups, lanes), 0)
    diag_ids = g_ids * PACK + lax.shift_right_logical(
        lax.broadcasted_iota(jnp.int32, (groups, lanes), 1), 5
    )

    def inside_rows(start, count):
        rows = first + start + lax.broadcasted_iota(jnp.int32, (count, 1, 1), 0)
        bound = jnp.where(rows >= 0, total - rows, 0)
        return (diag_ids[None] < bound).reshape(count * groups, lanes)

    def store(x_ref, h_ref, start, count, value):
        value = value.astype(jnp.bfloat16).astype(jnp.float32)
        x_ref[pl.ds(start, count)] = value.astype(jnp.bfloat16).reshape(count, groups, lanes)
        size = count * groups
        g_row = lax.broadcasted_iota(jnp.int32, (count, groups, 128), 1).reshape(size, 128)
        below = jnp.where(g_row == 0, 0.0, pltpu.roll(value[:, 128:], 1, 0))
        above = jnp.where(g_row == groups - 1, 0.0, pltpu.roll(value[:, :128], size - 1, 0))
        h_ref[pl.ds(start, count), :, :128] = below.astype(jnp.bfloat16).reshape(
            count, groups, 128
        )
        h_ref[pl.ds(start, count), :, 128:] = above.astype(jnp.bfloat16).reshape(
            count, groups, 128
        )

    def taps(x_ref, h_ref, start, count, step):
        pieces = []
        for along in (-1, 0, 1):
            at = start + along * step
            pieces.append(x_ref[pl.ds(at, count)].reshape(count * groups, lanes))
            pieces.append(h_ref[pl.ds(at, count)].reshape(count * groups, lanes))
        return jnp.concatenate(pieces, axis=1)

    def conv(x_ref, h_ref, mat, start, count, step):
        return jnp.dot(
            taps(x_ref, h_ref, start, count, step),
            mats[mat],
            preferred_element_type=jnp.float32,
        )

    width = 2 * lanes

    def diag_of(slot):
        return jnp.where(slot < 8, slot, jnp.where(slot < 12, slot - 12, slot - 4))

    delta = diag_of(
        lax.shift_right_logical(lax.broadcasted_iota(jnp.int32, (width, lanes), 0), 5)
    ) - lax.shift_right_logical(lax.broadcasted_iota(jnp.int32, (width, lanes), 1), 5)
    repeat = (
        lax.broadcasted_iota(jnp.int32, (32, lanes), 0)
        == lax.broadcasted_iota(jnp.int32, (32, lanes), 1) & 31
    ).astype(jnp.bfloat16)
    for mat, layer, sign, step in (
        (0, 0, 1, dil_one), (1, 1, 1, dil_two), (2, 1, -1, dil_two), (3, 0, -1, dil_one)
    ):
        for along in range(3):
            taken = along if sign > 0 else 2 - along
            total_mat = jnp.zeros((width, lanes), jnp.float32)
            for b in range(3):
                spread = lax.dot_general(
                    weights[layer, 3 * taken + b], repeat,
                    (((0 if sign > 0 else 1,), (0,)), ((), ())),
                    preferred_element_type=jnp.float32,
                )
                total_mat = jnp.where(
                    delta == sign * (b - 1) * step,
                    jnp.concatenate([spread] * 16, axis=0),
                    total_mat,
                )
            mats[mat, along * width : (along + 1) * width] = total_mat.astype(jnp.bfloat16)

    n0 = 4

    @pl.loop(0, (sub + 2 * HALO) // n0)
    def _(block):
        start = block * n0
        rows = []
        for u in range(n0):
            at = start + u
            halves = []
            for half in range(2):
                partner = right[half, pl.ds(at, groups, stride=PACK), :]
                halves.append(partner + left[half, pl.ds(at, 1), :])
            rows.append(jnp.concatenate(halves, axis=1) + bias[...])
        t = jnp.tanh(jnp.concatenate(rows, axis=0))
        keep = inside_rows(start, n0)
        s0[pl.ds(start, n0)] = (
            jnp.where(keep, 1.0 - t * t, 0.0).astype(jnp.bfloat16).reshape(n0, groups, lanes)
        )
        store(x0, h0, start, n0, jnp.where(keep, t, 0.0))

    @pl.loop(0, (sub + 6 * MAXDIL) // n1)
    def _(block):
        start = MAXDIL + block * n1
        t = jnp.tanh(conv(x0, h0, 0, start, n1, dil_one))
        keep = inside_rows(start, n1)
        s1[pl.ds(start, n1)] = (
            jnp.where(keep, 1.0 - t * t, 0.0).astype(jnp.bfloat16).reshape(n1, groups, lanes)
        )
        before = x0[pl.ds(start, n1)].reshape(n1 * groups, lanes).astype(jnp.float32)
        store(x1, h1, start, n1, jnp.where(keep, before + t, 0.0))

    @pl.loop(0, (sub + 4 * MAXDIL) // n2)
    def _(block):
        start = 2 * MAXDIL + block * n2
        t = jnp.tanh(conv(x1, h1, 1, start, n2, dil_two))
        t_high = t.astype(jnp.bfloat16)
        t_low = (t - t_high.astype(jnp.float32)).astype(jnp.bfloat16)
        scored = lax.dot_general(
            head[...], t_high, (((1,), (1,)), ((), ())), preferred_element_type=jnp.float32
        ) + lax.dot_general(
            head[...], t_low, (((1,), (1,)), ((), ())), preferred_element_type=jnp.float32
        )
        pred[block] = scored[:PACK] + scored[PACK:]
        factor = lax.dot_general(
            cots[block], expand[...], (((0,), (0,)), ((), ())),
            preferred_element_type=jnp.float32,
        )
        store(g2, hg2, start, n2, factor * (1.0 - t * t))

    def weight_grad(layer, g_ref, x_ref, h_ref, step):
        wacc[...] = jnp.zeros_like(wacc)

        @pl.loop(0, sub // n4)
        def _(block):
            start = HALO + block * n4
            wacc[...] += lax.dot_general(
                g_ref[pl.ds(start, n4)].reshape(n4 * groups, lanes),
                taps(x_ref, h_ref, start, n4, step),
                (((0,), (0,)), ((), ())),
                preferred_element_type=jnp.float32,
            )

        out_diag = lax.shift_right_logical(
            lax.broadcasted_iota(jnp.int32, (lanes, width), 0), 5
        )
        in_diag = diag_of(
            lax.shift_right_logical(lax.broadcasted_iota(jnp.int32, (lanes, width), 1), 5)
        )
        fold = (
            lax.broadcasted_iota(jnp.int32, (width, 32), 0) & 31
            == lax.broadcasted_iota(jnp.int32, (width, 32), 1)
        ).astype(jnp.float32)
        for a in range(3):
            product = wacc[:, a * width : (a + 1) * width]
            for b in range(3):
                picked = jnp.where(in_diag == out_diag + (b - 1) * step, product, 0.0)
                total_rows = picked[:32]
                for d in range(1, PACK):
                    total_rows = total_rows + picked[32 * d : 32 * (d + 1)]
                wgrad[layer, 3 * a + b] = jnp.dot(
                    total_rows, fold, precision=HIGHEST, preferred_element_type=jnp.float32
                )

    weight_grad(1, g2, x1, h1, dil_two)

    @pl.loop(0, (sub + 2 * MAXDIL) // n3)
    def _(block):
        start = 3 * MAXDIL + block * n3
        back = conv(g2, hg2, 2, start, n3, dil_two)
        b1[pl.ds(start, n3)] = back.reshape(n3, groups, lanes)
        scale = s1[pl.ds(start, n3)].reshape(n3 * groups, lanes).astype(jnp.float32)
        store(x1, h1, start, n3, back * scale)

    weight_grad(0, x1, x0, h0, dil_one)
    grad_right[...] = jnp.zeros_like(grad_right)

    @pl.loop(0, sub // n4)
    def _(block):
        start = HALO + block * n4
        back = conv(x1, h1, 3, start, n4, dil_one)
        scale = s0[pl.ds(start, n4)].reshape(n4 * groups, lanes).astype(jnp.float32)
        grad = (back + b1[pl.ds(start, n4)].reshape(n4 * groups, lanes)) * scale
        grad_left[block] = jnp.sum(grad.reshape(n4, groups, lanes), axis=1)
        for u in range(n4):
            at = pl.ds(block * n4 + u, groups, stride=PACK)
            for half in range(2):
                piece = grad[u * groups : (u + 1) * groups, 128 * half : 128 * (half + 1)]
                grad_right[half, at, :] = grad_right[half, at, :] + piece


def opening(
    plan, embeddings, projection, cot_in, projected, cot_out,
    low, high, cot_low, cot_high, parts, part_slots, cots, cot_slots, send, recv,
):
    n_bin, n_diag, sub, span, cot_span = plan
    me_bin, me_diag = lax.axis_index("bin"), lax.axis_index("diag")
    rows = embeddings.shape[1]
    after = {"bin": (me_bin + 1) % n_bin}
    before = {"bin": (me_bin + n_bin - 1) % n_bin}
    others = [{"diag": (me_diag + k) % n_diag} for k in range(1, n_diag)]
    barrier = pltpu.get_barrier_semaphore()
    for partner in others + [after, before]:
        pl.semaphore_signal(
            barrier, inc=1, device_id=partner, device_id_type=pl.DeviceIdType.MESH
        )
    pl.semaphore_wait(barrier, len(others) + 2)
    ids = iter(range(64))

    def copy(source, target, device):
        at = next(ids)
        made = pltpu.make_async_remote_copy(
            src_ref=source, dst_ref=target, send_sem=send.at[at], recv_sem=recv.at[at],
            device_id=device, device_id_type=pl.DeviceIdType.MESH,
        )
        made.start()
        return made

    first = [
        copy(embeddings, high, before),
        copy(embeddings.at[:, pl.ds(rows - 128, 128)], low, after),
    ]
    second = [
        copy(cot_in.at[:, pl.ds(0, 128)], cot_high, before),
        copy(cot_in.at[:, pl.ds(rows - 128, 128)], cot_low, after),
    ]
    has_low = (me_bin > 0).astype(jnp.float32)
    has_high = (me_bin < n_bin - 1).astype(jnp.float32)
    for made in first:
        made.wait()
    wide = jnp.concatenate(
        [
            low[...] * has_low.astype(jnp.bfloat16),
            embeddings[...],
            high[...] * has_high.astype(jnp.bfloat16),
        ],
        axis=1,
    )
    part = lax.dot_general(
        projection[...], wide, (((0,), (0,)), ((), ())), preferred_element_type=jnp.float32
    )
    for d in range(n_diag):
        at = 128 - HALO + d * sub
        parts[d, :, :span] = part[:, at : at + span]
        parts[d, :, span:] = jnp.zeros_like(parts[d, :, span:])
    moves = [
        copy(parts.at[(me_diag + k) % n_diag], part_slots.at[k - 1], others[k - 1])
        for k in range(1, n_diag)
    ]
    for made in second:
        made.wait()
    cot = jnp.concatenate(
        [cot_low[...] * has_low, cot_in[...], cot_high[...] * has_high], axis=1
    )
    for d in range(n_diag):
        at = 128 - 2 * MAXDIL + d * sub
        cots[d, :, :cot_span] = cot[:, at : at + cot_span]
        cots[d, :, cot_span:] = jnp.zeros_like(cots[d, :, cot_span:])
    cot_moves = [
        copy(cots.at[(me_diag + k) % n_diag], cot_slots.at[k - 1], others[k - 1])
        for k in range(1, n_diag)
    ]
    total = parts[me_diag]
    for k in range(1, n_diag):
        moves[k - 1].wait()
        total = total + part_slots[k - 1]
    projected[...] = jnp.transpose(total)
    cot_out[me_diag] = cots[me_diag]
    for k in range(1, n_diag):
        cot_moves[k - 1].wait()
        cot_out[(me_diag + n_diag - k) % n_diag] = cot_slots[k - 1]


def swapped(me, bit):
    return me + bit - 2 * bit * ((me // bit) % 2)


def tail(
    plan, both_in, conv_in, embeddings, projection, embed_out, proj_out, conv_out,
    both, both_slots, conv_slots, spill_slot, sums, cut_slot, held, sum_slots, far_slot,
    send, recv,
):
    n_bin, n_diag, rows, scaling = plan
    me_bin, me_diag = lax.axis_index("bin"), lax.axis_index("diag")
    diag_bits = [1 << k for k in range(n_diag.bit_length() - 1)]
    bin_bits = [1 << k for k in range(n_bin.bit_length() - 1)]
    after = {"bin": (me_bin + 1) % n_bin}
    before = {"bin": (me_bin + n_bin - 1) % n_bin}
    partners = [{"diag": swapped(me_diag, bit)} for bit in diag_bits]
    partners += [{"bin": swapped(me_bin, bit)} for bit in bin_bits]
    barrier = pltpu.get_barrier_semaphore()
    for partner in partners + [after, before]:
        pl.semaphore_signal(
            barrier, inc=1, device_id=partner, device_id_type=pl.DeviceIdType.MESH
        )
    pl.semaphore_wait(barrier, len(partners) + 2)

    near = partners[len(diag_bits)]
    ids = iter(range(64))
    count, half = conv_in.shape[0], both.shape[0] // 2

    def copy(source, target, at, device):
        return pltpu.make_async_remote_copy(
            src_ref=source, dst_ref=target, send_sem=send.at[at], recv_sem=recv.at[at],
            device_id=device, device_id_type=pl.DeviceIdType.MESH,
        )

    both[...] = both_in[...]
    sums[:count] = conv_in[...]
    mine, theirs = me_bin % 2, 1 - me_bin % 2
    conv_half, proj_half = count // 2, half

    def exchange(rows_at, size, slot, device):
        return copy(sums.at[pl.ds(rows_at, size)], slot, next(ids), device)

    conv_cut = exchange(theirs * conv_half, conv_half, cut_slot.at[pl.ds(0, conv_half)], near)
    conv_cut.start()
    for k in range(len(diag_bits)):
        first = copy(both, both_slots.at[k], next(ids), partners[k])
        first.start()
        first.wait()
        both[...] += both_slots[k]
    conv_cut.wait()
    held[:conv_half] = sums[pl.ds(mine * conv_half, conv_half)] + cut_slot[:conv_half]
    spill = both.shape[1] - rows
    hop = copy(both.at[pl.ds(half, half), pl.ds(rows, spill)], spill_slot, next(ids), after)
    hop.start()
    for k in range(len(diag_bits)):
        second = copy(
            held.at[pl.ds(0, conv_half)], conv_slots.at[k], next(ids), partners[k]
        )
        second.start()
        second.wait()
        held[:conv_half] += conv_slots[k]
    hop.wait()
    both[half:, :spill] += spill_slot[...]
    summed = both[:, :rows]
    part = lax.dot_general(
        summed, embeddings[...].astype(jnp.float32), (((1,), (1,)), ((), ())),
        precision=HIGHEST, preferred_element_type=jnp.float32,
    )
    features = part.shape[1]
    sums[count:] = jnp.zeros_like(sums[count:])
    sums[count:, :features] = part
    proj_cut = exchange(
        count + theirs * proj_half, proj_half, cut_slot.at[pl.ds(conv_half, proj_half)], near
    )
    proj_cut.start()
    embed_out[...] = lax.dot_general(
        projection[...].astype(jnp.float32), summed, (((1,), (0,)), ((), ())),
        precision=HIGHEST, preferred_element_type=jnp.float32,
    )
    proj_cut.wait()
    held[conv_half:] = (
        sums[pl.ds(count + mine * proj_half, proj_half)] + cut_slot[conv_half:]
    )
    for k in range(1, len(bin_bits)):
        step = copy(held, sum_slots.at[k - 1], next(ids), partners[len(diag_bits) + k])
        step.start()
        step.wait()
        held[...] += sum_slots[k - 1]
    last = copy(held, far_slot, next(ids), near)
    last.start()
    last.wait()
    own, far = held[...] * scaling, far_slot[...] * scaling
    conv_out[pl.ds(mine * conv_half, conv_half)] = own[:conv_half]
    conv_out[pl.ds(theirs * conv_half, conv_half)] = far[:conv_half]
    proj_out[pl.ds(mine * proj_half, proj_half)] = own[conv_half:, :features]
    proj_out[pl.ds(theirs * proj_half, proj_half)] = far[conv_half:, :features]


def split_two(x):
    high = x.astype(jnp.bfloat16)
    return high, (x - high.astype(jnp.float32)).astype(jnp.bfloat16)


def on_device(
    embeddings, projection, dist_bias, conv_weight, head_weight, dilations, band_limit, cotangent
):
    channels = conv_weight.shape[2]
    diag_dev, rows_dev = cotangent.shape
    n_bin, n_diag = lax.axis_size("bin"), lax.axis_size("diag")
    total_bins, diags = rows_dev * n_bin, diag_dev * n_diag
    me = lax.axis_index("diag")
    first_row = lax.axis_index("bin") * rows_dev
    sub = rows_dev // n_diag
    groups = diags // PACK
    lanes = PACK * channels
    reach = HALO + diags

    def pairs(k):
        return [(i, (i + k) % n_diag) for i in range(n_diag)]

    row_ids = first_row + jnp.arange(rows_dev, dtype=jnp.int32)[None, :]
    diag_ids = me * diag_dev + jnp.arange(diag_dev, dtype=jnp.int32)[:, None]
    counted = (row_ids + diag_ids < total_bins) & (diag_ids < band_limit[None, :])
    margin = 2 * MAXDIL
    span = sub + HALO + reach
    cot_span = sub + 2 * margin
    wide_span, wide_cot = -(-span // 128) * 128, -(-cot_span // 128) * 128
    features = embeddings.shape[0]
    vmem = pl.BlockSpec(memory_space=pltpu.VMEM)
    projected, cot = pl.pallas_call(
        functools.partial(opening, (n_bin, n_diag, sub, span, cot_span)),
        out_shape=[
            jax.ShapeDtypeStruct((wide_span, 2 * channels), jnp.float32),
            jax.ShapeDtypeStruct((n_diag, diag_dev, wide_cot), jnp.float32),
        ],
        in_specs=[vmem] * 3,
        out_specs=[vmem] * 2,
        scratch_shapes=[
            pltpu.VMEM((features, 128), jnp.bfloat16),
            pltpu.VMEM((features, rows_dev), jnp.bfloat16),
            pltpu.VMEM((diag_dev, 128), jnp.float32),
            pltpu.VMEM((diag_dev, 128), jnp.float32),
            pltpu.VMEM((n_diag, 2 * channels, wide_span), jnp.float32),
            pltpu.VMEM((n_diag - 1, 2 * channels, wide_span), jnp.float32),
            pltpu.VMEM((n_diag, diag_dev, wide_cot), jnp.float32),
            pltpu.VMEM((n_diag - 1, diag_dev, wide_cot), jnp.float32),
            pltpu.SemaphoreType.DMA((2 + 2 * n_diag,)),
            pltpu.SemaphoreType.DMA((2 + 2 * n_diag,)),
        ],
        compiler_params=pltpu.CompilerParams(collective_id=1, has_side_effects=True),
        name="opening",
    )(embeddings, projection, jnp.where(counted, cotangent, 0.0))
    cot = cot[:, :, :cot_span]
    region = sub + 2 * HALO
    reads = region + PACK * (groups - 1)
    left = jnp.tile(projected[:region, :channels], (1, PACK))
    right = jnp.concatenate(
        [projected[d : d + reads, channels:] for d in range(PACK)], axis=1
    )
    halves = lambda x: jnp.stack([x[:, : lanes // 2], x[:, lanes // 2 :]])
    bias = jnp.transpose(dist_bias.reshape(channels, groups, PACK), (1, 2, 0)).reshape(
        groups, lanes
    )

    n1 = cut(sub + 6 * MAXDIL, 36)
    n2 = cut(cot_span, 16)
    n3 = cut(sub + 2 * MAXDIL, 40)
    n4 = cut(sub, 32)
    blocks = cot_span // n2
    cot = jnp.transpose(cot.reshape(groups, PACK, blocks, n2), (2, 1, 3, 0)).reshape(
        blocks, PACK, n2 * groups
    )
    cot_high, cot_low = split_two(cot)
    head_high, head_low = split_two(head_weight)
    eye = jnp.eye(PACK, dtype=jnp.bfloat16)
    spread = lambda h: (eye[:, :, None] * h[None, None, :]).reshape(PACK, lanes)
    pad = jnp.zeros((PACK, lanes), jnp.bfloat16)
    cots = jnp.concatenate([cot_high, cot_low, cot_high, jnp.zeros_like(cot_high)], axis=1)
    expand = jnp.concatenate([spread(head_high), spread(head_high), spread(head_low), pad])
    head = jnp.concatenate([spread(head_high), spread(head_low)])
    info = jnp.concatenate([dilations, (first_row + me * sub - HALO)[None].astype(jnp.int32)])

    writes = sub + PACK * (groups - 1)
    full_map = pltpu.VMEM((region, groups, lanes), jnp.float32)
    half_map = pltpu.VMEM((region, groups, lanes), jnp.bfloat16)
    pred, grad_left, grad_right, conv_part = pl.pallas_call(
        functools.partial(kernel, (sub, groups, total_bins, n1, n2, n3, n4)),
        out_shape=[
            jax.ShapeDtypeStruct((blocks, PACK, n2 * groups), jnp.float32),
            jax.ShapeDtypeStruct((sub // n4, n4, lanes), jnp.float32),
            jax.ShapeDtypeStruct((2, writes, lanes // 2), jnp.float32),
            jax.ShapeDtypeStruct(conv_weight.shape, jnp.float32),
        ],
        in_specs=[pl.BlockSpec(memory_space=pltpu.SMEM)] + [vmem] * 7,
        out_specs=[vmem] * 4,
        scratch_shapes=[half_map] * 8
        + [
            full_map,
            pltpu.VMEM((lanes, 6 * lanes), jnp.float32),
            pltpu.VMEM((4, 6 * lanes, lanes), jnp.bfloat16),
        ],
        compiler_params=pltpu.CompilerParams(vmem_limit_bytes=60 * 1024 * 1024),
        name="band",
    )(info, halves(left), halves(right), bias, conv_weight, expand, head, cots)

    grad_right = jnp.concatenate([grad_right[0], grad_right[1]], axis=1)
    spilled = jnp.zeros((sub + diags, channels), jnp.float32)
    for d in range(PACK):
        spilled = spilled + jnp.pad(
            grad_right[:, d * channels : (d + 1) * channels],
            ((d, sub + diags - writes - d), (0, 0)),
        )
    lefts = jnp.sum(grad_left.reshape(sub, PACK, channels), axis=1)
    own = jnp.concatenate([jnp.pad(lefts, ((0, diags), (0, 0))), spilled], axis=1)
    buffer = lax.dynamic_update_slice_in_dim(
        jnp.zeros((rows_dev + diags, 2 * channels), jnp.float32), own, me * sub, 0
    )
    conv_rows = conv_part.size // 128
    scaling = 1.0 / math.sqrt(total_bins * diags)
    wide_both = (2 * channels, rows_dev + diags)
    diag_steps, bin_steps = n_diag.bit_length() - 1, n_bin.bit_length() - 1
    sum_rows = conv_rows + 2 * channels
    grad_embed, proj_sum, conv_sum = pl.pallas_call(
        functools.partial(tail, (n_bin, n_diag, rows_dev, scaling)),
        out_shape=[
            jax.ShapeDtypeStruct((features, rows_dev), jnp.float32),
            jax.ShapeDtypeStruct((2 * channels, features), jnp.float32),
            jax.ShapeDtypeStruct((conv_rows, 128), jnp.float32),
        ],
        in_specs=[vmem] * 4,
        out_specs=[vmem] * 3,
        scratch_shapes=[
            pltpu.VMEM(wide_both, jnp.float32),
            pltpu.VMEM((diag_steps,) + wide_both, jnp.float32),
            pltpu.VMEM((diag_steps, conv_rows // 2, 128), jnp.float32),
            pltpu.VMEM((channels, diags), jnp.float32),
            pltpu.VMEM((sum_rows, 128), jnp.float32),
            pltpu.VMEM((sum_rows // 2, 128), jnp.float32),
            pltpu.VMEM((sum_rows // 2, 128), jnp.float32),
            pltpu.VMEM((bin_steps - 1, sum_rows // 2, 128), jnp.float32),
            pltpu.VMEM((sum_rows // 2, 128), jnp.float32),
            pltpu.SemaphoreType.DMA((2 * diag_steps + bin_steps + 3,)),
            pltpu.SemaphoreType.DMA((2 * diag_steps + bin_steps + 3,)),
        ],
        compiler_params=pltpu.CompilerParams(collective_id=0, has_side_effects=True),
        name="tail",
    )(jnp.transpose(buffer), conv_part.reshape(conv_rows, 128), embeddings, projection)
    grad_proj = jnp.transpose(proj_sum)
    grad_conv = conv_sum.reshape(conv_part.shape)

    pred = jnp.transpose(pred.reshape(blocks, PACK, n2, groups), (3, 1, 0, 2)).reshape(
        diags, cot_span
    )[:, margin : margin + sub]
    pred_local = jnp.zeros((diag_dev, rows_dev), jnp.float32)
    for k in range(n_diag):
        other = lax.rem(me + k, n_diag)
        piece = lax.dynamic_slice_in_dim(pred, other * diag_dev, diag_dev, 0)
        if k:
            piece = lax.ppermute(piece, "diag", pairs(k))
        pred_local = lax.dynamic_update_slice_in_dim(
            pred_local, piece, lax.rem(me - k + n_diag, n_diag) * sub, 1
        )
    pred_local = jnp.where(counted, pred_local, 0.0)
    return (pred_local, grad_embed, grad_proj, grad_conv)


def solution(mesh):
    return jax.shard_map(
        on_device,
        mesh=mesh,
        in_specs=(
            P("diag", "bin"),
            P("diag", None),
            P(),
            P(),
            P(),
            P(),
            P("bin"),
            P("diag", "bin"),
        ),
        out_specs=(P("diag", "bin"), P("diag", "bin"), P("diag", None), P()),
        check_vma=False,
    )
```

```python
import functools
import math

import jax
import jax.numpy as jnp
from jax import lax
from jax.experimental import pallas as pl
from jax.experimental.pallas import tpu as pltpu
from jax.sharding import PartitionSpec as P

MAXDIL = 4
HALO = 4 * MAXDIL
PACK = 8


HIGHEST = lax.Precision.HIGHEST


def cut(rows, most):
    return max(n for n in range(1, most + 1) if rows % n == 0)


def kernel(
    plan, info, left, right, bias, weights, expand, head, cots, pred, grad_left, grad_right,
    wgrad, x0, h0, s0, x1, h1, s1, g2, hg2, b1, wacc, mats,
):
    sub, groups, total, n1, n2, n3, n4 = plan
    lanes = 256
    first = info[2]
    dil_one, dil_two = info[0], info[1]
    g_ids = lax.broadcasted_iota(jnp.int32, (groups, lanes), 0)
    diag_ids = g_ids * PACK + lax.shift_right_logical(
        lax.broadcasted_iota(jnp.int32, (groups, lanes), 1), 5
    )

    def inside_rows(start, count):
        rows = first + start + lax.broadcasted_iota(jnp.int32, (count, 1, 1), 0)
        bound = jnp.where(rows >= 0, total - rows, 0)
        return (diag_ids[None] < bound).reshape(count * groups, lanes)

    def store(x_ref, h_ref, start, count, value):
        value = value.astype(jnp.bfloat16).astype(jnp.float32)
        x_ref[pl.ds(start, count)] = value.astype(jnp.bfloat16).reshape(count, groups, lanes)
        size = count * groups
        g_row = lax.broadcasted_iota(jnp.int32, (count, groups, 128), 1).reshape(size, 128)
        below = jnp.where(g_row == 0, 0.0, pltpu.roll(value[:, 128:], 1, 0))
        above = jnp.where(g_row == groups - 1, 0.0, pltpu.roll(value[:, :128], size - 1, 0))
        h_ref[pl.ds(start, count), :, :128] = below.astype(jnp.bfloat16).reshape(
            count, groups, 128
        )
        h_ref[pl.ds(start, count), :, 128:] = above.astype(jnp.bfloat16).reshape(
            count, groups, 128
        )

    def taps(x_ref, h_ref, start, count, step):
        pieces = []
        for along in (-1, 0, 1):
            at = start + along * step
            pieces.append(x_ref[pl.ds(at, count)].reshape(count * groups, lanes))
            pieces.append(h_ref[pl.ds(at, count)].reshape(count * groups, lanes))
        return jnp.concatenate(pieces, axis=1)

    def conv(x_ref, h_ref, mat, start, count, step):
        return jnp.dot(
            taps(x_ref, h_ref, start, count, step),
            mats[mat],
            preferred_element_type=jnp.float32,
        )

    width = 2 * lanes

    def diag_of(slot):
        return jnp.where(slot < 8, slot, jnp.where(slot < 12, slot - 12, slot - 4))

    delta = diag_of(
        lax.shift_right_logical(lax.broadcasted_iota(jnp.int32, (width, lanes), 0), 5)
    ) - lax.shift_right_logical(lax.broadcasted_iota(jnp.int32, (width, lanes), 1), 5)
    repeat = (
        lax.broadcasted_iota(jnp.int32, (32, lanes), 0)
        == lax.broadcasted_iota(jnp.int32, (32, lanes), 1) & 31
    ).astype(jnp.bfloat16)
    for mat, layer, sign, step in (
        (0, 0, 1, dil_one), (1, 1, 1, dil_two), (2, 1, -1, dil_two), (3, 0, -1, dil_one)
    ):
        for along in range(3):
            taken = along if sign > 0 else 2 - along
            total_mat = jnp.zeros((width, lanes), jnp.float32)
            for b in range(3):
                spread = lax.dot_general(
                    weights[layer, 3 * taken + b], repeat,
                    (((0 if sign > 0 else 1,), (0,)), ((), ())),
                    preferred_element_type=jnp.float32,
                )
                total_mat = jnp.where(
                    delta == sign * (b - 1) * step,
                    jnp.concatenate([spread] * 16, axis=0),
                    total_mat,
                )
            mats[mat, along * width : (along + 1) * width] = total_mat.astype(jnp.bfloat16)

    n0 = 4

    @pl.loop(0, (sub + 2 * HALO) // n0)
    def _(block):
        start = block * n0
        rows = []
        for u in range(n0):
            at = start + u
            halves = []
            for half in range(2):
                partner = right[half, pl.ds(at, groups, stride=PACK), :]
                halves.append(partner + left[pl.ds(at, 1), :])
            rows.append(jnp.concatenate(halves, axis=1) + bias[...])
        t = jnp.tanh(jnp.concatenate(rows, axis=0))
        keep = inside_rows(start, n0)
        s0[pl.ds(start, n0)] = (
            jnp.where(keep, 1.0 - t * t, 0.0).astype(jnp.bfloat16).reshape(n0, groups, lanes)
        )
        store(x0, h0, start, n0, jnp.where(keep, t, 0.0))

    @pl.loop(0, (sub + 6 * MAXDIL) // n1)
    def _(block):
        start = MAXDIL + block * n1
        t = jnp.tanh(conv(x0, h0, 0, start, n1, dil_one))
        keep = inside_rows(start, n1)
        s1[pl.ds(start, n1)] = (
            jnp.where(keep, 1.0 - t * t, 0.0).astype(jnp.bfloat16).reshape(n1, groups, lanes)
        )
        before = x0[pl.ds(start, n1)].reshape(n1 * groups, lanes).astype(jnp.float32)
        store(x1, h1, start, n1, jnp.where(keep, before + t, 0.0))

    @pl.loop(0, (sub + 4 * MAXDIL) // n2)
    def _(block):
        start = 2 * MAXDIL + block * n2
        t = jnp.tanh(conv(x1, h1, 1, start, n2, dil_two))
        t_high = t.astype(jnp.bfloat16)
        t_low = (t - t_high.astype(jnp.float32)).astype(jnp.bfloat16)
        scored = lax.dot_general(
            head[...], t_high, (((1,), (1,)), ((), ())), preferred_element_type=jnp.float32
        ) + lax.dot_general(
            head[...], t_low, (((1,), (1,)), ((), ())), preferred_element_type=jnp.float32
        )
        pred[block] = scored[:PACK] + scored[PACK:]
        factor = lax.dot_general(
            cots[block], expand[...], (((0,), (0,)), ((), ())),
            preferred_element_type=jnp.float32,
        )
        store(g2, hg2, start, n2, factor * (1.0 - t * t))

    def weight_grad(layer, g_ref, x_ref, h_ref, step):
        wacc[...] = jnp.zeros_like(wacc)

        @pl.loop(0, sub // n4)
        def _(block):
            start = HALO + block * n4
            wacc[...] += lax.dot_general(
                g_ref[pl.ds(start, n4)].reshape(n4 * groups, lanes),
                taps(x_ref, h_ref, start, n4, step),
                (((0,), (0,)), ((), ())),
                preferred_element_type=jnp.float32,
            )

        out_diag = lax.shift_right_logical(
            lax.broadcasted_iota(jnp.int32, (lanes, width), 0), 5
        )
        in_diag = diag_of(
            lax.shift_right_logical(lax.broadcasted_iota(jnp.int32, (lanes, width), 1), 5)
        )
        fold = (
            lax.broadcasted_iota(jnp.int32, (width, 32), 0) & 31
            == lax.broadcasted_iota(jnp.int32, (width, 32), 1)
        ).astype(jnp.float32)
        for a in range(3):
            product = wacc[:, a * width : (a + 1) * width]
            for b in range(3):
                picked = jnp.where(in_diag == out_diag + (b - 1) * step, product, 0.0)
                total_rows = picked[:32]
                for d in range(1, PACK):
                    total_rows = total_rows + picked[32 * d : 32 * (d + 1)]
                wgrad[layer, 3 * a + b] = jnp.dot(
                    total_rows, fold, precision=HIGHEST, preferred_element_type=jnp.float32
                )

    weight_grad(1, g2, x1, h1, dil_two)

    @pl.loop(0, (sub + 2 * MAXDIL) // n3)
    def _(block):
        start = 3 * MAXDIL + block * n3
        back = conv(g2, hg2, 2, start, n3, dil_two)
        b1[pl.ds(start, n3)] = back.reshape(n3, groups, lanes)
        scale = s1[pl.ds(start, n3)].reshape(n3 * groups, lanes).astype(jnp.float32)
        store(x1, h1, start, n3, back * scale)

    weight_grad(0, x1, x0, h0, dil_one)
    grad_right[...] = jnp.zeros_like(grad_right)

    @pl.loop(0, sub // n4)
    def _(block):
        start = HALO + block * n4
        back = conv(x1, h1, 3, start, n4, dil_one)
        scale = s0[pl.ds(start, n4)].reshape(n4 * groups, lanes).astype(jnp.float32)
        grad = (back + b1[pl.ds(start, n4)].reshape(n4 * groups, lanes)) * scale
        grad_left[block] = jnp.sum(grad.reshape(n4, groups, lanes), axis=1)
        for u in range(n4):
            at = pl.ds(block * n4 + u, groups, stride=PACK)
            for half in range(2):
                piece = grad[u * groups : (u + 1) * groups, 128 * half : 128 * (half + 1)]
                grad_right[half, at, :] = grad_right[half, at, :] + piece


def opening(
    plan, embeddings, projection, cot_in, left, right, cot_out,
    low, high, cot_low, cot_high, parts, part_slots, cots, cot_slots, send, recv,
):
    n_bin, n_diag, sub, span, cot_span = plan
    me_bin, me_diag = lax.axis_index("bin"), lax.axis_index("diag")
    rows = embeddings.shape[1]
    after = {"bin": (me_bin + 1) % n_bin}
    before = {"bin": (me_bin + n_bin - 1) % n_bin}
    others = [{"diag": (me_diag + k) % n_diag} for k in range(1, n_diag)]
    barrier = pltpu.get_barrier_semaphore()
    for partner in others + [after, before]:
        pl.semaphore_signal(
            barrier, inc=1, device_id=partner, device_id_type=pl.DeviceIdType.MESH
        )
    pl.semaphore_wait(barrier, len(others) + 2)
    ids = iter(range(64))

    def copy(source, target, device):
        at = next(ids)
        made = pltpu.make_async_remote_copy(
            src_ref=source, dst_ref=target, send_sem=send.at[at], recv_sem=recv.at[at],
            device_id=device, device_id_type=pl.DeviceIdType.MESH,
        )
        made.start()
        return made

    first = [
        copy(embeddings, high, before),
        copy(embeddings.at[:, pl.ds(rows - 128, 128)], low, after),
    ]
    second = [
        copy(cot_in.at[:, pl.ds(0, 128)], cot_high, before),
        copy(cot_in.at[:, pl.ds(rows - 128, 128)], cot_low, after),
    ]
    has_low = (me_bin > 0).astype(jnp.float32)
    has_high = (me_bin < n_bin - 1).astype(jnp.float32)
    for made in first:
        made.wait()
    wide = jnp.concatenate(
        [
            low[...] * has_low.astype(jnp.bfloat16),
            embeddings[...],
            high[...] * has_high.astype(jnp.bfloat16),
        ],
        axis=1,
    )
    part = lax.dot_general(
        projection[...], wide, (((0,), (0,)), ((), ())), preferred_element_type=jnp.float32
    )
    for d in range(n_diag):
        at = 128 - HALO + d * sub
        parts[d, :, :span] = part[:, at : at + span]
        parts[d, :, span:] = jnp.zeros_like(parts[d, :, span:])
    moves = [
        copy(parts.at[(me_diag + k) % n_diag], part_slots.at[k - 1], others[k - 1])
        for k in range(1, n_diag)
    ]
    for made in second:
        made.wait()
    cot = jnp.concatenate(
        [cot_low[...] * has_low, cot_in[...], cot_high[...] * has_high], axis=1
    )
    for d in range(n_diag):
        at = 128 - 2 * MAXDIL + d * sub
        cots[d, :, :cot_span] = cot[:, at : at + cot_span]
        cots[d, :, cot_span:] = jnp.zeros_like(cots[d, :, cot_span:])
    cot_moves = [
        copy(cots.at[(me_diag + k) % n_diag], cot_slots.at[k - 1], others[k - 1])
        for k in range(1, n_diag)
    ]
    total = parts[me_diag]
    for k in range(1, n_diag):
        moves[k - 1].wait()
        total = total + part_slots[k - 1]
    channels = total.shape[0] // 2
    left[...] = jnp.transpose(jnp.concatenate([total[:channels]] * (PACK // 2), axis=0))
    turned = [
        total[channels:] if d == 0 else pltpu.roll(total[channels:], total.shape[1] - d, 1)
        for d in range(PACK)
    ]
    for h in range(2):
        part = turned[h * PACK // 2 : (h + 1) * PACK // 2]
        right[h] = jnp.transpose(jnp.concatenate(part, axis=0))
    cot_out[me_diag] = cots[me_diag]
    for k in range(1, n_diag):
        cot_moves[k - 1].wait()
        cot_out[(me_diag + n_diag - k) % n_diag] = cot_slots[k - 1]


def swapped(me, bit):
    return me + bit - 2 * bit * ((me // bit) % 2)


def tail(
    plan, left_in, right_in, conv_in, embeddings, projection, embed_out, proj_out, conv_out,
    both, both_slots, conv_slots, spill_slot, sums, cut_slot, held, sum_slots, far_slot,
    send, recv,
):
    n_bin, n_diag, rows, scaling = plan
    me_bin, me_diag = lax.axis_index("bin"), lax.axis_index("diag")
    diag_bits = [1 << k for k in range(n_diag.bit_length() - 1)]
    bin_bits = [1 << k for k in range(n_bin.bit_length() - 1)]
    after = {"bin": (me_bin + 1) % n_bin}
    before = {"bin": (me_bin + n_bin - 1) % n_bin}
    partners = [{"diag": swapped(me_diag, bit)} for bit in diag_bits]
    partners += [{"bin": swapped(me_bin, bit)} for bit in bin_bits]
    barrier = pltpu.get_barrier_semaphore()
    for partner in partners + [after, before]:
        pl.semaphore_signal(
            barrier, inc=1, device_id=partner, device_id_type=pl.DeviceIdType.MESH
        )
    pl.semaphore_wait(barrier, len(partners) + 2)

    near = partners[len(diag_bits)]
    ids = iter(range(64))
    count, half = conv_in.shape[0], both.shape[0] // 2
    sub, reach = left_in.shape[0], left_in.shape[0] + both.shape[1] - rows

    def copy(source, target, at, device):
        return pltpu.make_async_remote_copy(
            src_ref=source, dst_ref=target, send_sem=send.at[at], recv_sem=recv.at[at],
            device_id=device, device_id_type=pl.DeviceIdType.MESH,
        )

    both[...] = jnp.zeros_like(both)
    fold = (
        lax.broadcasted_iota(jnp.int32, (half, PACK * half), 0)
        == lax.broadcasted_iota(jnp.int32, (half, PACK * half), 1) & (half - 1)
    ).astype(jnp.float32)
    lefts = lax.dot_general(
        fold, left_in[...], (((1,), (1,)), ((), ())),
        precision=HIGHEST, preferred_element_type=jnp.float32,
    )
    rights = jnp.zeros((half, right_in.shape[1]), jnp.float32)
    for h in range(2):
        turned = jnp.transpose(right_in[h])
        for q in range(PACK // 2):
            d = h * PACK // 2 + q
            piece = turned[q * half : (q + 1) * half]
            rights = rights + (pltpu.roll(piece, d, 1) if d else piece)
    for d in range(n_diag):
        @pl.when(me_diag == d)
        def _():
            both[:half, d * sub : (d + 1) * sub] = lefts
            both[half:, d * sub : d * sub + reach] = rights[:, :reach]

    sums[:count] = conv_in[...]
    mine, theirs = me_bin % 2, 1 - me_bin % 2
    conv_half, proj_half = count // 2, half

    def exchange(rows_at, size, slot, device):
        return copy(sums.at[pl.ds(rows_at, size)], slot, next(ids), device)

    conv_cut = exchange(theirs * conv_half, conv_half, cut_slot.at[pl.ds(0, conv_half)], near)
    conv_cut.start()
    for k in range(len(diag_bits)):
        first = copy(both, both_slots.at[k], next(ids), partners[k])
        first.start()
        first.wait()
        both[...] += both_slots[k]
    conv_cut.wait()
    held[:conv_half] = sums[pl.ds(mine * conv_half, conv_half)] + cut_slot[:conv_half]
    spill = both.shape[1] - rows
    hop = copy(both.at[pl.ds(half, half), pl.ds(rows, spill)], spill_slot, next(ids), after)
    hop.start()
    for k in range(len(diag_bits)):
        second = copy(
            held.at[pl.ds(0, conv_half)], conv_slots.at[k], next(ids), partners[k]
        )
        second.start()
        second.wait()
        held[:conv_half] += conv_slots[k]
    hop.wait()
    both[half:, :spill] += spill_slot[...]
    summed = both[:, :rows]
    part = lax.dot_general(
        summed, embeddings[...].astype(jnp.float32), (((1,), (1,)), ((), ())),
        precision=HIGHEST, preferred_element_type=jnp.float32,
    )
    features = part.shape[1]
    sums[count:] = jnp.zeros_like(sums[count:])
    sums[count:, :features] = part
    proj_cut = exchange(
        count + theirs * proj_half, proj_half, cut_slot.at[pl.ds(conv_half, proj_half)], near
    )
    proj_cut.start()
    embed_out[...] = lax.dot_general(
        projection[...].astype(jnp.float32), summed, (((1,), (0,)), ((), ())),
        precision=HIGHEST, preferred_element_type=jnp.float32,
    )
    proj_cut.wait()
    held[conv_half:] = (
        sums[pl.ds(count + mine * proj_half, proj_half)] + cut_slot[conv_half:]
    )
    for k in range(1, len(bin_bits)):
        step = copy(held, sum_slots.at[k - 1], next(ids), partners[len(diag_bits) + k])
        step.start()
        step.wait()
        held[...] += sum_slots[k - 1]
    last = copy(held, far_slot, next(ids), near)
    last.start()
    last.wait()
    own, far = held[...] * scaling, far_slot[...] * scaling
    conv_out[pl.ds(mine * conv_half, conv_half)] = own[:conv_half]
    conv_out[pl.ds(theirs * conv_half, conv_half)] = far[:conv_half]
    proj_out[pl.ds(mine * proj_half, proj_half)] = own[conv_half:, :features]
    proj_out[pl.ds(theirs * proj_half, proj_half)] = far[conv_half:, :features]


def split_two(x):
    high = x.astype(jnp.bfloat16)
    return high, (x - high.astype(jnp.float32)).astype(jnp.bfloat16)


def on_device(
    embeddings, projection, dist_bias, conv_weight, head_weight, dilations, band_limit, cotangent
):
    channels = conv_weight.shape[2]
    diag_dev, rows_dev = cotangent.shape
    n_bin, n_diag = lax.axis_size("bin"), lax.axis_size("diag")
    total_bins, diags = rows_dev * n_bin, diag_dev * n_diag
    me = lax.axis_index("diag")
    first_row = lax.axis_index("bin") * rows_dev
    sub = rows_dev // n_diag
    groups = diags // PACK
    lanes = PACK * channels
    reach = HALO + diags

    def pairs(k):
        return [(i, (i + k) % n_diag) for i in range(n_diag)]

    row_ids = first_row + jnp.arange(rows_dev, dtype=jnp.int32)[None, :]
    diag_ids = me * diag_dev + jnp.arange(diag_dev, dtype=jnp.int32)[:, None]
    counted = (row_ids + diag_ids < total_bins) & (diag_ids < band_limit[None, :])
    margin = 2 * MAXDIL
    span = sub + HALO + reach
    cot_span = sub + 2 * margin
    wide_span, wide_cot = -(-span // 128) * 128, -(-cot_span // 128) * 128
    features = embeddings.shape[0]
    vmem = pl.BlockSpec(memory_space=pltpu.VMEM)
    left, right, cot = pl.pallas_call(
        functools.partial(opening, (n_bin, n_diag, sub, span, cot_span)),
        out_shape=[
            jax.ShapeDtypeStruct((wide_span, lanes // 2), jnp.float32),
            jax.ShapeDtypeStruct((2, wide_span, lanes // 2), jnp.float32),
            jax.ShapeDtypeStruct((n_diag, diag_dev, wide_cot), jnp.float32),
        ],
        in_specs=[vmem] * 3,
        out_specs=[vmem] * 3,
        scratch_shapes=[
            pltpu.VMEM((features, 128), jnp.bfloat16),
            pltpu.VMEM((features, rows_dev), jnp.bfloat16),
            pltpu.VMEM((diag_dev, 128), jnp.float32),
            pltpu.VMEM((diag_dev, 128), jnp.float32),
            pltpu.VMEM((n_diag, 2 * channels, wide_span), jnp.float32),
            pltpu.VMEM((n_diag - 1, 2 * channels, wide_span), jnp.float32),
            pltpu.VMEM((n_diag, diag_dev, wide_cot), jnp.float32),
            pltpu.VMEM((n_diag - 1, diag_dev, wide_cot), jnp.float32),
            pltpu.SemaphoreType.DMA((2 + 2 * n_diag,)),
            pltpu.SemaphoreType.DMA((2 + 2 * n_diag,)),
        ],
        compiler_params=pltpu.CompilerParams(collective_id=1, has_side_effects=True),
        name="opening",
    )(embeddings, projection, jnp.where(counted, cotangent, 0.0))
    cot = cot[:, :, :cot_span]
    region = sub + 2 * HALO
    bias = jnp.transpose(dist_bias.reshape(channels, groups, PACK), (1, 2, 0)).reshape(
        groups, lanes
    )

    n1 = cut(sub + 6 * MAXDIL, 36)
    n2 = cut(cot_span, 16)
    n3 = cut(sub + 2 * MAXDIL, 40)
    n4 = cut(sub, 32)
    blocks = cot_span // n2
    cot = jnp.transpose(cot.reshape(groups, PACK, blocks, n2), (2, 1, 3, 0)).reshape(
        blocks, PACK, n2 * groups
    )
    cot_high, cot_low = split_two(cot)
    head_high, head_low = split_two(head_weight)
    eye = jnp.eye(PACK, dtype=jnp.bfloat16)
    spread = lambda h: (eye[:, :, None] * h[None, None, :]).reshape(PACK, lanes)
    pad = jnp.zeros((PACK, lanes), jnp.bfloat16)
    cots = jnp.concatenate([cot_high, cot_low, cot_high, jnp.zeros_like(cot_high)], axis=1)
    expand = jnp.concatenate([spread(head_high), spread(head_high), spread(head_low), pad])
    head = jnp.concatenate([spread(head_high), spread(head_low)])
    info = jnp.concatenate([dilations, (first_row + me * sub - HALO)[None].astype(jnp.int32)])

    writes = -(-(sub + diags) // 128) * 128
    full_map = pltpu.VMEM((region, groups, lanes), jnp.float32)
    half_map = pltpu.VMEM((region, groups, lanes), jnp.bfloat16)
    pred, grad_left, grad_right, conv_part = pl.pallas_call(
        functools.partial(kernel, (sub, groups, total_bins, n1, n2, n3, n4)),
        out_shape=[
            jax.ShapeDtypeStruct((blocks, PACK, n2 * groups), jnp.float32),
            jax.ShapeDtypeStruct((sub // n4, n4, lanes), jnp.float32),
            jax.ShapeDtypeStruct((2, writes, lanes // 2), jnp.float32),
            jax.ShapeDtypeStruct(conv_weight.shape, jnp.float32),
        ],
        in_specs=[pl.BlockSpec(memory_space=pltpu.SMEM)] + [vmem] * 7,
        out_specs=[vmem] * 4,
        scratch_shapes=[half_map] * 8
        + [
            full_map,
            pltpu.VMEM((lanes, 6 * lanes), jnp.float32),
            pltpu.VMEM((4, 6 * lanes, lanes), jnp.bfloat16),
        ],
        compiler_params=pltpu.CompilerParams(vmem_limit_bytes=60 * 1024 * 1024),
        name="band",
    )(info, left, right, bias, conv_weight, expand, head, cots)

    conv_rows = conv_part.size // 128
    scaling = 1.0 / math.sqrt(total_bins * diags)
    wide_both = (2 * channels, rows_dev + diags)
    diag_steps, bin_steps = n_diag.bit_length() - 1, n_bin.bit_length() - 1
    sum_rows = conv_rows + 2 * channels
    grad_embed, proj_sum, conv_sum = pl.pallas_call(
        functools.partial(tail, (n_bin, n_diag, rows_dev, scaling)),
        out_shape=[
            jax.ShapeDtypeStruct((features, rows_dev), jnp.float32),
            jax.ShapeDtypeStruct((2 * channels, features), jnp.float32),
            jax.ShapeDtypeStruct((conv_rows, 128), jnp.float32),
        ],
        in_specs=[vmem] * 5,
        out_specs=[vmem] * 3,
        scratch_shapes=[
            pltpu.VMEM(wide_both, jnp.float32),
            pltpu.VMEM((diag_steps,) + wide_both, jnp.float32),
            pltpu.VMEM((diag_steps, conv_rows // 2, 128), jnp.float32),
            pltpu.VMEM((channels, diags), jnp.float32),
            pltpu.VMEM((sum_rows, 128), jnp.float32),
            pltpu.VMEM((sum_rows // 2, 128), jnp.float32),
            pltpu.VMEM((sum_rows // 2, 128), jnp.float32),
            pltpu.VMEM((bin_steps - 1, sum_rows // 2, 128), jnp.float32),
            pltpu.VMEM((sum_rows // 2, 128), jnp.float32),
            pltpu.SemaphoreType.DMA((2 * diag_steps + bin_steps + 3,)),
            pltpu.SemaphoreType.DMA((2 * diag_steps + bin_steps + 3,)),
        ],
        compiler_params=pltpu.CompilerParams(collective_id=0, has_side_effects=True),
        name="tail",
    )(
        grad_left.reshape(sub, lanes), grad_right, conv_part.reshape(conv_rows, 128),
        embeddings, projection,
    )
    grad_proj = jnp.transpose(proj_sum)
    grad_conv = conv_sum.reshape(conv_part.shape)

    pred = jnp.transpose(pred.reshape(blocks, PACK, n2, groups), (3, 1, 0, 2)).reshape(
        diags, cot_span
    )[:, margin : margin + sub]
    pieces = []
    for k in range(n_diag):
        other = lax.rem(me + k, n_diag)
        piece = lax.dynamic_slice_in_dim(pred, other * diag_dev, diag_dev, 0)
        pieces.append(lax.ppermute(piece, "diag", pairs(k)) if k else piece)
    columns = []
    for d in range(n_diag):
        source = lax.rem(me - d + n_diag, n_diag)
        chosen = pieces[0]
        for k in range(1, n_diag):
            chosen = jnp.where(source == k, pieces[k], chosen)
        columns.append(chosen)
    pred_local = jnp.concatenate(columns, axis=1)
    pred_local = jnp.where(counted, pred_local, 0.0)
    return (pred_local, grad_embed, grad_proj, grad_conv)


def solution(mesh):
    return jax.shard_map(
        on_device,
        mesh=mesh,
        in_specs=(
            P("diag", "bin"),
            P("diag", None),
            P(),
            P(),
            P(),
            P(),
            P("bin"),
            P("diag", "bin"),
        ),
        out_specs=(P("diag", "bin"), P("diag", "bin"), P("diag", None), P()),
        check_vma=False,
    )
```
